128 devices in a mesh: dom: 128 (over x, z, y, core).
Axes of the slice: x: 4, y: 4, z: 4, core: 2. Of those that a mesh axis runs over, the one named last changes fastest.
Arguments:
- adjoint_start: float32 [3, 884736], P(None, 'dom'), may hold values from -6 to 6
- adjoint_source: float32 [3, 884736], P(None, 'dom'), may hold values from -6 to 6
- inverse_diagonal: float32 [3, 884736], P(None, 'dom'), may hold values from 0.05 to 0.3
- primal_field: float32 [3, 884736], P(None, 'dom'), may hold values from -6 to 6
- cell_load: float32 [192, 32768], P(None, 'dom'), may hold values from -6 to 6
- modulus: float32 [32768], P('dom'), may hold values from 0.5 to 4
- stiffness: float32 [192, 192], replicated
- connectivity: int32 [64, 32768], P(None, 'dom'), may hold values from 0 to 16368
- hang_node: int32 [16384], P('dom'), may hold values from 0 to 16368, as said below
- hang_master: int32 [16, 16384], P(None, 'dom'), may hold values from 0 to 16368
- hang_weight: float32 [16, 16384], P(None, 'dom'), may hold values from -0.25 to 0.45
- ghost_lists: int32 [8, 32768], P(None, 'dom'), may hold values from 0 to 16368
- subface_cell: int32 [8, 16384], P(None, 'dom'), may hold values from 0 to 255
- subface_face: int32 [8, 16384], P(None, 'dom'), may hold values from 0 to 5
- subface_owner: int32 [8, 16384], P(None, 'dom'), may hold values from 0 to 256, as said below
Outputs:
- adjoint: float32 [3, 884736], P(None, 'dom')
- indicator: float32 [32768], P('dom')
The draws below stay inside these ranges and needn't reach their ends.
Inputs may be any that keep to these rules, and one draw needn't show every extreme that they name: `hang_node`: on each partition the live hanging slots come first and hold distinct codes under min(16368, 6912); all slots after them hold 16368; between half and all of a partition's slots are live. `subface_owner`: 256 marks an unused slot; between half and all of each neighbour slot's entries are live.
All inputs are finite; a program needn't handle non-finite values.
Results may differ from the reference program's by a relative error of at most 0.0003.
Values sent between devices are 32-bit elements; how exact they have to be, the bound alone decides.
A program may use at most 64 MiB of HBM per device.

```python
import math
import jax
import jax.numpy as jnp
from jax import lax

C = 256
LOC = 192
MASTERS = 16
REACH = 4
SWEEPS = 2
NODES_DEV = 6912
GHOST = 256
SUBS = 128
HANG = 128
EXT = 8960
CELLS = 32768
NODES = 884736
N_DOM = 128


def draw_stiffness(key, part):
    key = jax.random.fold_in(key, 11)
    first_key, second_key = jax.random.split(key)
    diagonal = jax.random.uniform(first_key, (LOC, LOC), jnp.float32, 1.5, 2.5)
    spread = jax.random.normal(second_key, (LOC, LOC), jnp.float32) * (0.8 / LOC ** 0.5)
    rows = lax.broadcasted_iota(jnp.int32, (LOC, LOC), 0)
    cols = lax.broadcasted_iota(jnp.int32, (LOC, LOC), 1)
    return jnp.where(rows == cols, diagonal, spread)


def draw_hang_node(key, part):
    key = jax.random.fold_in(key, 12)
    keys = jax.random.split(key, N_DOM + 1)
    bound = min(16368, NODES_DEV)

    def pick_one(single):
        return jax.random.permutation(single, bound)[:HANG].astype(jnp.int32)
    picks = jax.vmap(pick_one)(keys[1:])
    counts = jax.random.randint(keys[0], (N_DOM,), HANG // 2, HANG)
    counts = counts.at[0].set(HANG // 2)
    slots = jnp.arange(HANG, dtype=jnp.int32)
    chosen = jnp.where(slots[None, :] < counts[:, None], picks, 16368)
    return chosen.reshape(-1).astype(jnp.int32)


def draw_subface_owner(key, part):
    key = jax.random.fold_in(key, 13)
    first_key, second_key = jax.random.split(key)
    owners = jax.random.randint(first_key, (N_DOM, 2 * REACH, SUBS), 0, C)
    counts = jax.random.randint(second_key, (N_DOM, 2 * REACH), SUBS // 2, SUBS + 1)
    counts = counts.at[0, 0].set(SUBS // 2).at[1, 0].set(SUBS)
    slots = jnp.arange(SUBS, dtype=jnp.int32)
    chosen = jnp.where(slots[None, None, :] < counts[:, :, None], owners, C)
    return jnp.transpose(chosen, (1, 0, 2)).reshape(2 * REACH, N_DOM * SUBS).astype(jnp.int32)


def plant(values, stream_key, low, largest):
    place = [jax.random.randint(jax.random.fold_in(stream_key, axis), (), 0, length) for axis, length in enumerate(values.shape)]
    longest = values.shape.index(max(values.shape))
    next_to = place[:longest] + [(place[longest] + 1) % values.shape[longest]] + place[longest + 1:]
    return values.at[tuple(place)].set(low).at[tuple(next_to)].set(largest)


def steps_of(rng, extent, cuts, least, top_value):
    level, own = 1.0, jax.random.fold_in(rng, 6)
    for dim, shards_of in cuts:
        heights = jnp.exp(jax.random.uniform(jax.random.fold_in(own, dim), (shards_of,), jnp.float32, least / len(cuts), top_value / len(cuts)))
        level = level * jnp.repeat(heights, extent[dim] // shards_of).reshape([-1 if axis == dim else 1 for axis in range(len(extent))])
    return level


def scatter_about(stream_key, shape, deviation, reach, cuts=(), kind=jnp.bfloat16):
    result = jax.random.normal(stream_key, shape, jnp.float32) * deviation
    if len(cuts) > 0:
        result = steps_of(stream_key, shape, cuts, -0.22, 0.18) * result
    return jnp.clip(result, min=-reach, max=reach).astype(kind)


def setup_inputs(seed: int = 0) -> dict:
    key_of = jax.random.split(jax.random.key(seed), 16)
    adjoint_start = scatter_about(key_of[0], (3, NODES), 1.0, 6.0, ((1, 128),), jnp.float32)
    adjoint_source = scatter_about(key_of[1], (3, NODES), 1.0, 6.0, ((1, 128),), jnp.float32)
    inverse_diagonal = jnp.clip(jnp.exp(math.log(0.3) - 1.7917595 * jax.random.uniform(key_of[2], (3, NODES), jnp.float32) ** steps_of(key_of[2], (3, NODES), ((1, 128),), -0.2, 0.2)), 0.05, 0.3)
    primal_field = scatter_about(key_of[3], (3, NODES), 1.0, 6.0, ((1, 128),), jnp.float32)
    cell_load = scatter_about(key_of[4], (LOC, CELLS), 1.0, 6.0, ((1, 128),), jnp.float32)
    modulus = jnp.clip(jnp.exp(math.log(4.0) - 2.0794415 * jax.random.uniform(key_of[5], (CELLS,), jnp.float32) ** steps_of(key_of[5], (CELLS,), ((0, 128),), -0.2, 0.2)), 0.5, 4.0)
    stiffness = draw_stiffness(jax.random.fold_in(key_of[15], 71), 0)
    connectivity = plant(jax.random.randint(key_of[7], (64, CELLS), 0, 16369), jax.random.fold_in(key_of[7], 1), 0, 16368).astype(jnp.int32)
    hang_node = draw_hang_node(jax.random.fold_in(key_of[15], 71), 0)
    hang_master = plant(jax.random.randint(key_of[9], (MASTERS, HANG * N_DOM), 0, 16369), jax.random.fold_in(key_of[9], 1), 0, 16368).astype(jnp.int32)
    hang_weight = jnp.clip(-0.25 + 0.7 * jax.random.uniform(key_of[10], (MASTERS, HANG * N_DOM), jnp.float32) ** steps_of(key_of[10], (MASTERS, HANG * N_DOM), ((1, 128),), -0.2, 0.2), -0.25, 0.45)
    ghost_lists = plant(jax.random.randint(key_of[11], (2 * REACH, GHOST * N_DOM), 0, 16369), jax.random.fold_in(key_of[11], 1), 0, 16368).astype(jnp.int32)
    subface_cell = plant(jax.random.randint(key_of[12], (2 * REACH, SUBS * N_DOM), 0, C), jax.random.fold_in(key_of[12], 1), 0, C - 1).astype(jnp.int32)
    subface_face = plant(jax.random.randint(key_of[13], (2 * REACH, SUBS * N_DOM), 0, 6), jax.random.fold_in(key_of[13], 1), 0, 5).astype(jnp.int32)
    subface_owner = draw_subface_owner(jax.random.fold_in(key_of[15], 71), 0)
    return {"adjoint_start": adjoint_start, "adjoint_source": adjoint_source, "inverse_diagonal": inverse_diagonal, "primal_field": primal_field, "cell_load": cell_load, "modulus": modulus, "stiffness": stiffness, "connectivity": connectivity, "hang_node": hang_node, "hang_master": hang_master, "hang_weight": hang_weight, "ghost_lists": ghost_lists, "subface_cell": subface_cell, "subface_face": subface_face, "subface_owner": subface_owner}


relaxation = 0.7
scale_down = 16.0
pad_code = 16368


def neighbour_offsets():
    return [step + 1 for step in range(REACH)] + [-(step + 1) for step in range(REACH)]


def by_device(array):
    lead = array.shape[:-1]
    width = array.shape[-1] // N_DOM
    return jnp.moveaxis(array.reshape(lead + (N_DOM, width)), -2, 0)


def to_global(array):
    moved = jnp.moveaxis(array, 0, -2)
    return moved.reshape(moved.shape[:-2] + (-1,))


def decode_connect(codes):
    cells = jnp.arange(codes.shape[-1], dtype=jnp.int32)
    return ((27 * cells + 17 * codes) % EXT).astype(jnp.int32)


def decode_master(codes):
    slots = jnp.arange(codes.shape[-1], dtype=jnp.int32)
    return ((17 * codes + 8 * slots) % EXT).astype(jnp.int32)


def decode_node(codes):
    return jnp.where(codes == pad_code, EXT, (13 * codes) % NODES_DEV).astype(jnp.int32)


def decode_lists(codes):
    slots = jnp.arange(codes.shape[-1], dtype=jnp.int32)
    return ((17 * codes + slots) % NODES_DEV).astype(jnp.int32)


def move_along(blocks, direction):
    pieces = []
    for slot, offset in enumerate(neighbour_offsets()):
        amount = direction * offset
        block = blocks[:, slot]
        empty = jnp.zeros_like(block[:abs(amount)])
        if amount > 0:
            pieces.append(jnp.concatenate([empty, block[:-amount]], 0))
        else:
            pieces.append(jnp.concatenate([block[-amount:], empty], 0))
    return jnp.stack(pieces, 1)


def face_table(width):
    node = jnp.arange(width, dtype=jnp.int32) % 64
    first = node // 16
    second = (node // 4) % 4
    third = node % 4
    rows = [first == 0, first == 3, second == 0, second == 3, third == 0, third == 3]
    return jnp.stack(rows).astype(jnp.float32)


def constrain(extended, node, master, weight):
    padded = jnp.concatenate([extended, jnp.zeros((extended.shape[0], 1), extended.dtype)], 1)
    values = jnp.sum(weight[None] * padded[:, master], axis=1)
    padded = padded.at[:, node].set(values)
    return padded[:, :-1]


def release(totals, node, master, weight):
    padded = jnp.concatenate([totals, jnp.zeros((totals.shape[0], 1), totals.dtype)], 1)
    held = padded[:, node]
    padded = padded.at[:, node].set(0.0)
    spread = weight[None] * held[:, None, :]
    padded = padded.at[:, master.reshape(-1)].add(spread.reshape(totals.shape[0], -1))
    return padded[:, :-1]


def local_product(extended, connect, modulus, stiffness, node, master, weight):
    fixed = constrain(extended, node, master, weight)
    cells = fixed[:, connect].reshape(3 * connect.shape[0], -1)
    image = modulus[None] * lax.dot_general(stiffness, cells, (((0,), (0,)), ((), ())), precision=lax.Precision.HIGHEST)
    totals = jnp.zeros_like(fixed).at[:, connect].add(image.reshape(3, connect.shape[0], -1))
    return release(totals, node, master, weight)


def cell_section(adjoint_ext, primal_ext, connect, modulus, stiffness, node, master, weight, load, sub_cell, sub_face):
    adjoint_cells = constrain(adjoint_ext, node, master, weight)[:, connect].reshape(3 * connect.shape[0], -1)
    primal_cells = constrain(primal_ext, node, master, weight)[:, connect].reshape(3 * connect.shape[0], -1)
    applied = modulus[None] * jnp.dot(stiffness, primal_cells, precision=lax.Precision.HIGHEST)
    cell_term = jnp.sum(adjoint_cells * (load - applied), axis=0)
    flux = jnp.dot(face_table(applied.shape[0]), applied * adjoint_cells, precision=lax.Precision.HIGHEST)
    count = connect.shape[1]
    sent = flux.reshape(-1)[sub_face * count + sub_cell]
    return cell_term, sent


def reference(adjoint_start, adjoint_source, inverse_diagonal, primal_field, cell_load, modulus, stiffness, connectivity, hang_node, hang_master, hang_weight, ghost_lists, subface_cell, subface_face, subface_owner):
    adjoint = by_device(adjoint_start)
    source = by_device(adjoint_source)
    inverse = by_device(inverse_diagonal)
    primal = by_device(primal_field)
    load = by_device(cell_load)
    moduli = by_device(modulus)
    connect = decode_connect(by_device(connectivity))
    node = decode_node(by_device(hang_node))
    master = decode_master(by_device(hang_master))
    weight = by_device(hang_weight)
    lists = decode_lists(by_device(ghost_lists))
    sub_cell = by_device(subface_cell)
    sub_face = by_device(subface_face)
    sub_owner = by_device(subface_owner)
    owned_count = adjoint.shape[2]
    ghost_count = lists.shape[2]

    def import_all(owned):
        blocks = jax.vmap(lambda values, rows: jnp.moveaxis(values[:, rows], 1, 0))(owned, lists)
        ghosts = move_along(blocks, 1)
        ghosts = jnp.moveaxis(ghosts, 1, 2).reshape(N_DOM, owned.shape[1], -1)
        return jnp.concatenate([owned, ghosts], 2)

    def product_one(items):
        return local_product(items[0], items[1], items[2], stiffness, items[3], items[4], items[5])

    for sweep in range(SWEEPS):
        extended = import_all(adjoint)
        totals = lax.map(product_one, (extended, connect, moduli, node, master, weight))
        owned_part = totals[:, :, :owned_count]
        ghost_part = jnp.moveaxis(totals[:, :, owned_count:].reshape(N_DOM, 3, 2 * REACH, ghost_count), 2, 1)
        back = move_along(ghost_part, -1)

        def add_back(values, rows, returned):
            return values.at[:, rows.reshape(-1)].add(jnp.moveaxis(returned, 0, 1).reshape(3, -1))

        applied = jax.vmap(add_back)(owned_part, lists, back)
        adjoint = adjoint + relaxation * inverse * (source - applied)

    adjoint_ext = import_all(adjoint)
    primal_ext = import_all(primal)

    def section_one(items):
        return cell_section(items[0], items[1], items[2], items[3], stiffness, items[4], items[5], items[6], items[7], items[8], items[9])

    cell_term, sent = lax.map(section_one, (adjoint_ext, primal_ext, connect, moduli, node, master, weight, load, sub_cell, sub_face))
    received = move_along(sent, 1)
    cell_count = connect.shape[2]

    def collect(owners, values):
        return jnp.zeros((cell_count + 1,), values.dtype).at[owners.reshape(-1)].add(values.reshape(-1))[:cell_count]

    face_term = jax.vmap(collect)(sub_owner, received)
    indicator = (jnp.abs(cell_term) + jnp.abs(face_term)) / scale_down
    return to_global(adjoint), indicator.reshape(-1)
```

```python
import jax
import jax.numpy as jnp
from jax import lax
from jax.experimental import pallas as pl
from jax.experimental.pallas import tpu as pltpu
from jax.sharding import PartitionSpec as P

MESH = pl.DeviceIdType.MESH
F32 = jnp.float32
BF16 = jnp.bfloat16

REACH = 4
SLOTS = 2 * REACH
SWEEPS = 2
NODES_DEV = 6912
EXT = 8960
PAD_CODE = 16368
RELAXATION = 0.7

LANES = 256
OWNED = 27
GHOST_ROW = 32
ROWS = 40
OFFSETS = [step + 1 for step in range(REACH)] + [-(step + 1) for step in range(REACH)]


def modulo(values, divisor):
    quotient = ((values.astype(F32) + 0.5) * (1.0 / divisor)).astype(jnp.int32)
    return values - quotient * divisor


def place(slots):
    row = slots >> 8
    return row + jnp.where(row >= OWNED, GHOST_ROW - OWNED, 0), slots & 255


def one_hot(row, count, dtype):
    spots = lax.broadcasted_iota(jnp.int32, (count, row.shape[1]), 0)
    return jnp.where(spots == row, 1.0, 0.0).astype(dtype)


def halves(values):
    high = values.astype(BF16).astype(F32)
    return jnp.concatenate([high, values - high], 0).astype(BF16)


def dot(a, b):
    return jnp.dot(a, b, preferred_element_type=F32)


def dot_nt(a, b):
    return lax.dot_general(a, b, (((1,), (1,)), ((), ())), preferred_element_type=F32)


def dot_tn(a, b):
    return lax.dot_general(a, b, (((0,), (0,)), ((), ())), preferred_element_type=F32)


def joined(values):
    half = values.shape[0] // 2
    return values[:half] + values[half:]


def picked(table, lane_hot, row_hot, parts, rows):
    found = joined(dot(table, lane_hot))
    return [
        jnp.sum(found[part * rows : (part + 1) * rows] * row_hot, axis=0, keepdims=True)
        for part in range(parts)
    ]


def spread(values, row_hot):
    return halves(jnp.concatenate([row_hot * value for value in values], 0))


def kernel(
    start_ref,
    source_ref,
    inverse_ref,
    primal_ref,
    load_ref,
    modulus_ref,
    stiff_ref,
    connect_ref,
    node_ref,
    master_ref,
    weight_ref,
    lists_ref,
    sub_cell_ref,
    sub_face_ref,
    sub_owner_ref,
    adjoint_ref,
    indicator_ref,
    table,
    primal_table,
    source,
    inverse,
    row_hots,
    lane_hots,
    list_rows,
    list_lanes,
    master_rows,
    master_lanes,
    node_rows,
    node_lanes,
    keep,
    sub_rows,
    sub_lanes,
    owner_lanes,
    cells,
    image,
    primal_cells,
    send_first,
    recv_first,
    send_ghost,
    recv_ghost,
    send_sub,
    recv_sub,
    send_sem,
    recv_sem,
):
    me = lax.axis_index("dom")
    count = lax.axis_size("dom")

    def device(offset):
        return lax.rem(me + offset + count, count)

    barrier = pltpu.get_barrier_semaphore()
    for offset in OFFSETS:
        pl.semaphore_signal(barrier, inc=1, device_id=(device(offset),), device_id_type=MESH)

    def exchange(send, recv, turn, direction):
        copies = []
        for slot, offset in enumerate(OFFSETS):
            copies.append(
                pltpu.make_async_remote_copy(
                    src_ref=send.at[slot],
                    dst_ref=recv.at[slot],
                    send_sem=send_sem.at[turn, slot],
                    recv_sem=recv_sem.at[turn, slot],
                    device_id=(device(direction * offset),),
                    device_id_type=MESH,
                )
            )
        for copy in copies:
            copy.start()
        return copies

    def arrived(slot, direction, values):
        origin = me - direction * OFFSETS[slot]
        inside = jnp.logical_and(origin >= 0, origin < count)
        return jnp.where(inside, values, 0.0)

    table[...] = jnp.zeros_like(table)
    primal_table[...] = jnp.zeros_like(primal_table)
    source[...] = jnp.zeros_like(source)
    inverse[...] = jnp.zeros_like(inverse)
    for part in range(3):
        for row in range(OWNED):
            spot = pl.ds(row * LANES, LANES)
            table[part * ROWS + row, :] = start_ref[part, spot]
            primal_table[part * ROWS + row, :] = primal_ref[part, spot]
            source[part * GHOST_ROW + row, :] = source_ref[part, spot]
            inverse[part * GHOST_ROW + row, :] = inverse_ref[part, spot]

    lane_ids = lax.broadcasted_iota(jnp.int32, (SLOTS, LANES), 1)
    lists = modulo(17 * lists_ref[...] + lane_ids, NODES_DEV)
    for slot in range(SLOTS):
        row = lists[slot : slot + 1]
        spot = pl.ds(slot * LANES, LANES)
        list_lanes[:, spot] = one_hot(row & 255, LANES, BF16)
        list_rows[:, spot] = one_hot(row >> 8, GHOST_ROW, F32)

    def owned_of(ref):
        return jnp.concatenate(
            [ref[pl.ds(part * ROWS, GHOST_ROW), :] for part in range(3)], 0
        )

    def export(values, send, parts):
        stacked = halves(values)
        for slot in range(SLOTS):
            spot = pl.ds(slot * LANES, LANES)
            rows = picked(stacked, list_lanes[:, spot], list_rows[:, spot], parts, GHOST_ROW)
            for part in range(parts):
                send[slot, 2 * part : 2 * part + 1, :] = rows[part][:, :128]
                send[slot, 2 * part + 1 : 2 * part + 2, :] = rows[part][:, 128:]

    def import_into(ref, recv, first):
        for slot in range(SLOTS):
            block = arrived(slot, 1, recv[slot])
            for part in range(3):
                spot = 2 * (first + part)
                ref[pl.ds(part * ROWS + GHOST_ROW + slot, 1), pl.ds(0, 128)] = block[
                    spot : spot + 1
                ]
                ref[pl.ds(part * ROWS + GHOST_ROW + slot, 1), pl.ds(128, 128)] = block[
                    spot + 1 : spot + 2
                ]

    export(jnp.concatenate([owned_of(table), owned_of(primal_table)], 0), send_first, 6)
    pl.semaphore_wait(barrier, SLOTS)
    pending = exchange(send_first, recv_first, 0, 1)

    def build(block, carry):
        rows = connect_ref[pl.ds(pl.multiple_of(block * 8, 8), 8), :]
        row_ids, lanes = place(modulo(17 * rows + 27 * lane_ids, EXT))
        for step in range(8):
            spot = pl.ds(step * LANES, LANES)
            lane_hots[block, :, spot] = one_hot(lanes[step : step + 1], LANES, BF16)
            row_hots[block, :, spot] = one_hot(row_ids[step : step + 1], ROWS, F32)
        return carry

    lax.fori_loop(0, 8, build, 0)

    hang_ids = lax.broadcasted_iota(jnp.int32, (16, 128), 1)
    row_ids, lanes = place(modulo(17 * master_ref[...] + 8 * hang_ids, EXT))
    weight = weight_ref[...]
    for step in range(16):
        spot = pl.ds(step * 128, 128)
        master_lanes[:, spot] = one_hot(lanes[step : step + 1], LANES, BF16)
        master_rows[:, spot] = (
            one_hot(row_ids[step : step + 1], ROWS, F32) * weight[step : step + 1]
        )
    node = node_ref[...]
    spots = modulo(13 * node, NODES_DEV)
    hang_row = jnp.where(node == PAD_CODE, -1, spots >> 8)
    node_lanes[...] = one_hot(spots & 255, LANES, BF16)
    node_rows[...] = one_hot(hang_row, ROWS, F32)
    keep[...] = 1.0 - dot_nt(one_hot(hang_row, 48, BF16), node_lanes[...])[:ROWS]
    for slot in range(SLOTS):
        spot = pl.ds(slot * 128, 128)
        sub_lanes[:, spot] = one_hot(sub_cell_ref[slot : slot + 1, :], LANES, BF16)
        sub_rows[:, spot] = one_hot(sub_face_ref[slot : slot + 1, :], 8, F32)
        owner_lanes[:, spot] = one_hot(sub_owner_ref[slot : slot + 1, :], LANES, BF16)

    stiff = stiff_ref[...]
    stiff_high = stiff.astype(BF16)
    stiff_low = (stiff - stiff_high.astype(F32)).astype(BF16)
    modulus = modulus_ref[...]

    def kept(values):
        return jnp.concatenate(
            [values[part * ROWS : (part + 1) * ROWS] * keep[...] for part in range(3)], 0
        )

    def constrain(values):
        stacked = halves(values)
        totals = [jnp.zeros((8, LANES), F32)] * 3
        for step in range(8):
            spot = pl.ds(step * LANES, LANES)
            found = joined(dot(stacked, master_lanes[:, spot]))
            for part in range(3):
                term = found[part * ROWS : (part + 1) * ROWS] * master_rows[:, spot]
                for group in range(ROWS // 8):
                    totals[part] = totals[part] + term[group * 8 : group * 8 + 8]
        sums = [jnp.sum(total, axis=0, keepdims=True) for total in totals]
        sums = [each[:, :128] + each[:, 128:] for each in sums]
        written = joined(dot_nt(spread(sums, node_rows[...]), node_lanes[...]))
        return kept(values) + written

    def gather_cells(values, out):
        stacked = halves(values)

        def body(block, carry):
            found = [[], [], []]
            for step in range(8):
                spot = pl.ds(step * LANES, LANES)
                rows = picked(
                    stacked, lane_hots[block, :, spot], row_hots[block, :, spot], 3, ROWS
                )
                for part in range(3):
                    found[part].append(rows[part])
            for part in range(3):
                spot = pl.ds(pl.multiple_of(part * 64 + block * 8, 8), 8)
                out[spot, :] = jnp.concatenate(found[part], 0)
            return carry

        lax.fori_loop(0, 8, body, 0)

    def scatter_cells(values):
        def body(block, total):
            columns = []
            rows = [
                values[pl.ds(pl.multiple_of(part * 64 + block * 8, 8), 8), :] for part in range(3)
            ]
            for step in range(8):
                spot = pl.ds(step * LANES, LANES)
                row_hot = row_hots[block, :, spot]
                columns.append(spread([each[step : step + 1] for each in rows], row_hot))
            return total + dot_nt(jnp.concatenate(columns, 1), lane_hots[block])

        total = lax.fori_loop(0, 8, body, jnp.zeros((6 * ROWS, LANES), F32))
        return joined(total)

    def release(totals):
        held = picked(halves(totals), node_lanes[...], node_rows[...], 3, ROWS)
        held = [jnp.concatenate([each, each], 1) for each in held]
        columns = []
        for step in range(8):
            spot = pl.ds(step * LANES, LANES)
            columns.append(spread(held, master_rows[:, spot]))
        added = joined(dot_nt(jnp.concatenate(columns, 1), master_lanes[...]))
        return kept(totals) + added

    def product(left_high, left_low, values, form):
        high = values.astype(BF16)
        low = (values - high.astype(F32)).astype(BF16)
        return form(left_high, high) + form(left_high, low) + form(left_low, high)

    for copy in pending:
        copy.wait()
    import_into(table, recv_first, 0)
    import_into(primal_table, recv_first, 3)

    for sweep in range(SWEEPS):
        if sweep:
            export(owned_of(table), send_ghost.at[2 * sweep - 1], 3)
            for copy in exchange(
                send_ghost.at[2 * sweep - 1], recv_ghost.at[2 * sweep - 1], 2 * sweep, 1
            ):
                copy.wait()
            import_into(table, recv_ghost.at[2 * sweep - 1], 0)
        gather_cells(constrain(table[...]), cells)
        image[...] = modulus * product(stiff_high, stiff_low, cells[...], dot_tn)
        totals = release(scatter_cells(image))
        send, recv = send_ghost.at[2 * sweep], recv_ghost.at[2 * sweep]
        for slot in range(SLOTS):
            for part in range(3):
                spot = part * ROWS + GHOST_ROW + slot
                send[slot, 2 * part : 2 * part + 1, :] = totals[spot : spot + 1, :128]
                send[slot, 2 * part + 1 : 2 * part + 2, :] = totals[spot : spot + 1, 128:]
        pending = exchange(send, recv, 2 * sweep + 1, -1)
        if sweep == 0:
            gather_cells(constrain(primal_table[...]), primal_cells)
            primal_cells[...] = modulus * product(
                stiff_high, stiff_low, primal_cells[...], dot
            )
        for copy in pending:
            copy.wait()
        columns = []
        for slot in range(SLOTS):
            block = arrived(slot, -1, recv[slot])
            rows = [
                jnp.concatenate([block[2 * part : 2 * part + 1], block[2 * part + 1 : 2 * part + 2]], 1)
                for part in range(3)
            ]
            columns.append(spread(rows, list_rows[:, pl.ds(slot * LANES, LANES)]))
        returned = joined(dot_nt(jnp.concatenate(columns, 1), list_lanes[...]))
        for part in range(3):
            owned = pl.ds(part * ROWS, GHOST_ROW)
            span = pl.ds(part * GHOST_ROW, GHOST_ROW)
            applied = (
                totals[part * ROWS : part * ROWS + GHOST_ROW]
                + returned[part * GHOST_ROW : (part + 1) * GHOST_ROW]
            )
            table[owned, :] = table[owned, :] + RELAXATION * inverse[span, :] * (
                source[span, :] - applied
            )

    last = 2 * SWEEPS - 1
    export(owned_of(table), send_ghost.at[last], 3)
    pending = exchange(send_ghost.at[last], recv_ghost.at[last], 2 * SWEEPS, 1)
    for part in range(3):
        for row in range(OWNED):
            adjoint_ref[part, pl.ds(row * LANES, LANES)] = table[part * ROWS + row, :]
    for copy in pending:
        copy.wait()
    import_into(table, recv_ghost.at[last], 0)
    gather_cells(constrain(table[...]), cells)

    applied = primal_cells[...]
    adjoint_cells = cells[...]
    cell_term = jnp.sum(adjoint_cells * (load_ref[...] - applied), axis=0, keepdims=True)
    work = applied * adjoint_cells
    face = lax.broadcasted_iota(jnp.int32, (16, 192), 0)
    node_id = lax.broadcasted_iota(jnp.int32, (16, 192), 1) & 63
    first, second, third = node_id >> 4, (node_id >> 2) & 3, node_id & 3
    axis_index = jnp.where(face < 2, first, jnp.where(face < 4, second, third))
    on_face = jnp.logical_and(face < 6, axis_index == 3 * (face & 1))
    faces = jnp.where(on_face, 1.0, 0.0).astype(BF16)
    work_high = work.astype(BF16)
    work_low = (work - work_high.astype(F32)).astype(BF16)
    flux = (dot(faces, work_high) + dot(faces, work_low))[:8]
    sent = jnp.sum(joined(dot(halves(flux), sub_lanes[...])) * sub_rows[...], axis=0, keepdims=True)
    for slot in range(SLOTS):
        send_sub[slot] = sent[:, slot * 128 : (slot + 1) * 128]
    for copy in exchange(send_sub, recv_sub, 2 * SWEEPS + 1, 1):
        copy.wait()
    received = jnp.concatenate(
        [arrived(slot, 1, recv_sub[slot]) for slot in range(SLOTS)], 1
    )
    stacked = halves(jnp.broadcast_to(received, (8, SLOTS * 128)))
    face_term = dot_nt(stacked, owner_lanes[...])
    face_term = face_term[0:1] + face_term[8:9]
    indicator_ref[...] = (jnp.abs(cell_term) + jnp.abs(face_term)) * (1.0 / 16.0)


def local(
    adjoint_start,
    adjoint_source,
    inverse_diagonal,
    primal_field,
    cell_load,
    modulus,
    stiffness,
    connectivity,
    hang_node,
    hang_master,
    hang_weight,
    ghost_lists,
    subface_cell,
    subface_face,
    subface_owner,
):
    turns = 2 * SWEEPS + 2
    vmem = pltpu.VMEM
    adjoint, indicator = pl.pallas_call(
        kernel,
        out_shape=(
            jax.ShapeDtypeStruct((3, NODES_DEV), F32),
            jax.ShapeDtypeStruct((1, LANES), F32),
        ),
        in_specs=[pl.BlockSpec(memory_space=pltpu.VMEM)] * 15,
        out_specs=(pl.BlockSpec(memory_space=pltpu.VMEM),) * 2,
        scratch_shapes=[
            vmem((3 * ROWS, LANES), F32),
            vmem((3 * ROWS, LANES), F32),
            vmem((3 * GHOST_ROW, LANES), F32),
            vmem((3 * GHOST_ROW, LANES), F32),
            vmem((8, ROWS, 8 * LANES), F32),
            vmem((8, LANES, 8 * LANES), BF16),
            vmem((GHOST_ROW, SLOTS * LANES), F32),
            vmem((LANES, SLOTS * LANES), BF16),
            vmem((ROWS, 16 * 128), F32),
            vmem((LANES, 16 * 128), BF16),
            vmem((ROWS, 128), F32),
            vmem((LANES, 128), BF16),
            vmem((ROWS, LANES), F32),
            vmem((8, SLOTS * 128), F32),
            vmem((LANES, SLOTS * 128), BF16),
            vmem((LANES, SLOTS * 128), BF16),
            vmem((192, LANES), F32),
            vmem((192, LANES), F32),
            vmem((192, LANES), F32),
            vmem((SLOTS, 12, 128), F32),
            vmem((SLOTS, 12, 128), F32),
            vmem((2 * SWEEPS, SLOTS, 6, 128), F32),
            vmem((2 * SWEEPS, SLOTS, 6, 128), F32),
            vmem((SLOTS, 1, 128), F32),
            vmem((SLOTS, 1, 128), F32),
            pltpu.SemaphoreType.DMA((turns, SLOTS)),
            pltpu.SemaphoreType.DMA((turns, SLOTS)),
        ],
        compiler_params=pltpu.CompilerParams(
            collective_id=0, has_side_effects=True, vmem_limit_bytes=56 * 1024 * 1024
        ),
    )(
        adjoint_start,
        adjoint_source,
        inverse_diagonal,
        primal_field,
        cell_load,
        modulus.reshape(1, LANES),
        stiffness,
        connectivity,
        hang_node.reshape(1, 128),
        hang_master,
        hang_weight,
        ghost_lists,
        subface_cell,
        subface_face,
        subface_owner,
    )
    return adjoint, indicator.reshape(LANES)


def solution(mesh):
    wide, flat = P(None, "dom"), P("dom")
    placed = (wide,) * 5 + (flat, P(), wide, flat) + (wide,) * 6
    return jax.shard_map(
        local, mesh=mesh, in_specs=placed, out_specs=(wide, flat), check_vma=False
    )
```

```python
import jax
import jax.numpy as jnp
from jax import lax
from jax.experimental import pallas as pl
from jax.experimental.pallas import tpu as pltpu
from jax.sharding import PartitionSpec as P

MESH = pl.DeviceIdType.MESH
F32 = jnp.float32
BF16 = jnp.bfloat16

REACH = 4
SLOTS = 2 * REACH
SWEEPS = 2
NODES_DEV = 6912
EXT = 8960
PAD_CODE = 16368
RELAXATION = 0.7
BUILD_FIRST = 4
PRIMAL_FIRST = 4

LANES = 256
OWNED = 27
HANG_ROW = 27
GHOST_ROW = 32
ROWS = 40
OFFSETS = [step + 1 for step in range(REACH)] + [-(step + 1) for step in range(REACH)]


def modulo(values, divisor):
    quotient = ((values.astype(F32) + 0.5) * (1.0 / divisor)).astype(jnp.int32)
    return values - quotient * divisor


def place(slots):
    row = slots >> 8
    return row + jnp.where(row >= OWNED, GHOST_ROW - OWNED, 0), slots & 255


def one_hot(row, count, dtype):
    spots = lax.broadcasted_iota(jnp.int32, (count, row.shape[1]), 0)
    return jnp.where(spots == row, 1.0, 0.0).astype(dtype)


def halves(values):
    high = values.astype(BF16).astype(F32)
    return jnp.concatenate([high, values - high], 0).astype(BF16)


def dot(a, b):
    return jnp.dot(a, b, preferred_element_type=F32)


def dot_nt(a, b):
    return lax.dot_general(a, b, (((1,), (1,)), ((), ())), preferred_element_type=F32)


def dot_tn(a, b):
    return lax.dot_general(a, b, (((0,), (0,)), ((), ())), preferred_element_type=F32)


def joined(values):
    half = values.shape[0] // 2
    return values[:half] + values[half:]


def picked(table, lane_hot, row_hot, parts, rows):
    found = joined(dot(table, lane_hot))
    return [
        jnp.sum(found[part * rows : (part + 1) * rows] * row_hot, axis=0, keepdims=True)
        for part in range(parts)
    ]


def spread(values, row_hot):
    return halves(jnp.concatenate([row_hot * value for value in values], 0))


def kernel(*refs):
    operands, outputs, refs = refs[:15], refs[15:17], refs[17:]
    staged, refs = refs[:15], refs[15:]
    (
        start_ref,
        source_ref,
        inverse_ref,
        primal_ref,
        load_ref,
        modulus_ref,
        stiff_ref,
        connect_ref,
        node_ref,
        master_ref,
        weight_ref,
        lists_ref,
        sub_cell_ref,
        sub_face_ref,
        sub_owner_ref,
    ) = staged
    adjoint_ref, indicator_ref = outputs
    (
        table,
        primal_table,
        source,
        inverse,
        ghosts,
        row_hots,
        lane_hots,
        list_rows,
        list_lanes,
        master_rows,
        master_lanes,
        sub_rows,
        sub_lanes,
        owner_lanes,
        owned_cells,
        cells,
        image,
        primal_cells,
        primal_stack,
        send_first,
        recv_first,
        send_ghost,
        recv_ghost,
        send_sub,
        recv_sub,
        send_sem,
        recv_sem,
        load_sem,
    ) = refs
    me = lax.axis_index("dom")
    count = lax.axis_size("dom")

    def exists(offset):
        other = me + offset
        return jnp.logical_and(other >= 0, other < count)

    barrier = pltpu.get_barrier_semaphore()
    for offset in OFFSETS:

        @pl.when(exists(offset))
        def _(offset=offset):
            pl.semaphore_signal(
                barrier, inc=1, device_id=(me + offset,), device_id_type=MESH
            )

    loads = [
        pltpu.make_async_copy(operands[k], staged[k], load_sem.at[k]) for k in range(15)
    ]
    for k in (11, 0, 3, 7, 8, 9, 10, 1, 2, 6, 5, 12, 13, 14, 4):
        loads[k].start()

    sent = []

    def exchange(send, recv, turn, direction):
        copies = []
        for slot, offset in enumerate(OFFSETS):
            away = direction * offset
            copy = pltpu.make_async_remote_copy(
                src_ref=send.at[slot],
                dst_ref=recv.at[slot],
                send_sem=send_sem.at[turn, slot],
                recv_sem=recv_sem.at[turn, slot],
                device_id=(me + away,),
                device_id_type=MESH,
            )
            pl.when(exists(away))(copy.start)
            copies.append((-away, copy))
            sent.append((away, copy))
        return copies

    def finish(copies):
        for away, copy in copies:
            pl.when(exists(away))(copy.wait_recv)

    def arrived(slot, direction, values):
        return jnp.where(exists(-direction * OFFSETS[slot]), values, 0.0)

    def owned_of(ref):
        return jnp.concatenate(
            [ref[part * ROWS : part * ROWS + GHOST_ROW, :] for part in range(3)], 0
        )

    def fill(ref, rows, values):
        for part in range(3):
            ref[part * rows + OWNED : part * rows + GHOST_ROW, :] = jnp.zeros(
                (GHOST_ROW - OWNED, LANES), F32
            )
            for row in range(OWNED):
                ref[part * rows + row : part * rows + row + 1, :] = values[
                    part : part + 1, row * LANES : (row + 1) * LANES
                ]

    lane_ids = lax.broadcasted_iota(jnp.int32, (SLOTS, LANES), 1)
    loads[11].wait()
    lists = modulo(17 * lists_ref[...] + lane_ids, NODES_DEV)
    for slot in range(SLOTS):
        row = lists[slot : slot + 1]
        spot = pl.ds(slot * LANES, LANES)
        list_lanes[:, spot] = one_hot(row & 255, LANES, BF16)
        list_rows[:, spot] = one_hot(row >> 8, GHOST_ROW, F32)
    loads[0].wait()
    fill(table, GHOST_ROW, start_ref)
    loads[3].wait()
    fill(primal_table, ROWS, primal_ref)

    def export(values, send, parts):
        stacked = halves(values)
        for slot in range(SLOTS):
            spot = pl.ds(slot * LANES, LANES)
            rows = picked(stacked, list_lanes[:, spot], list_rows[:, spot], parts, GHOST_ROW)
            for part in range(parts):
                send[slot, 2 * part : 2 * part + 1, :] = rows[part][:, :128]
                send[slot, 2 * part + 1 : 2 * part + 2, :] = rows[part][:, 128:]

    def imported(recv, first):
        for slot in range(SLOTS):
            block = arrived(slot, 1, recv[slot])
            for part in range(3):
                spot = 2 * (first + part)
                row = pl.ds(part * SLOTS + slot, 1)
                ghosts[row, pl.ds(0, 128)] = block[spot : spot + 1]
                ghosts[row, pl.ds(128, 128)] = block[spot + 1 : spot + 2]
        return ghosts[...]

    export(jnp.concatenate([table[...], owned_of(primal_table)], 0), send_first, 6)

    for k in (7, 8, 9, 10):
        loads[k].wait()
    node = node_ref[...]
    spots = modulo(13 * node, NODES_DEV)
    hang_row = jnp.where(node == PAD_CODE, -1, spots >> 8)
    numbers = (lax.broadcasted_iota(jnp.int32, (1, 128), 1) + 1).astype(F32)
    marks = dot_nt(
        (one_hot(hang_row, GHOST_ROW, F32) * numbers).astype(BF16),
        one_hot(spots & 255, LANES, BF16),
    ).astype(BF16)

    def build(block, carry):
        codes = connect_ref[pl.ds(pl.multiple_of(block * 8, 8), 8), :]
        rows, lanes = place(modulo(17 * codes + 27 * lane_ids, EXT))
        numbers = []
        for step in range(8):
            found = dot(marks, one_hot(lanes[step : step + 1], LANES, BF16))
            found = found * one_hot(rows[step : step + 1], GHOST_ROW, F32)
            numbers.append(jnp.sum(found, axis=0, keepdims=True))
        number = jnp.concatenate(numbers, 0).astype(jnp.int32)
        rows = jnp.where(number > 0, HANG_ROW, rows)
        lanes = jnp.where(number > 0, number - 1, lanes)
        for step in range(8):
            spot = pl.ds(step * LANES, LANES)
            lane_hots[block, :, spot] = one_hot(lanes[step : step + 1], LANES, BF16)
            row_hots[block, :, spot] = one_hot(rows[step : step + 1], ROWS, F32)
        return carry

    lax.fori_loop(0, BUILD_FIRST, build, 0)
    peers = jnp.minimum(me, REACH) + jnp.minimum(count - 1 - me, REACH)
    pl.semaphore_wait(barrier, peers)

    pending = exchange(send_first, recv_first, 0, 1)
    lax.fori_loop(BUILD_FIRST, 8, build, 0)

    hang_ids = lax.broadcasted_iota(jnp.int32, (16, 128), 1)
    row_ids, lanes = place(modulo(17 * master_ref[...] + 8 * hang_ids, EXT))
    weight = weight_ref[...]
    for step in range(16):
        spot = pl.ds(step * 128, 128)
        master_lanes[:, spot] = one_hot(lanes[step : step + 1], LANES, BF16)
        master_rows[:, spot] = (
            one_hot(row_ids[step : step + 1], ROWS, F32) * weight[step : step + 1]
        )

    def masters(values, low, rows):
        stacked = halves(values)
        totals = [jnp.zeros((8, LANES), F32)] * 3
        for step in range(8):
            spot = pl.ds(step * LANES, LANES)
            found = joined(dot(stacked, master_lanes[:, spot]))
            for part in range(3):
                term = found[part * rows : (part + 1) * rows] * master_rows[low : low + rows, spot]
                for group in range(rows // 8):
                    totals[part] = totals[part] + term[group * 8 : group * 8 + 8]
        sums = [jnp.sum(total, axis=0, keepdims=True) for total in totals]
        return [each[:, :128] + each[:, 128:] for each in sums]

    def hanging(first, second):
        rows = [a + b for a, b in zip(first, second)]
        rows = jnp.concatenate(rows + [jnp.zeros((5, 128), F32)], 0)
        return jnp.concatenate([rows, jnp.zeros((8, 128), F32)], 1)

    def gather_rows(stacked, rows, out, first, end):
        def body(block, carry):
            found = [[], [], []]
            for step in range(8):
                spot = pl.ds(step * LANES, LANES)
                values = picked(
                    stacked, lane_hots[block, :, spot], row_hots[block, :rows, spot], 3, rows
                )
                for part in range(3):
                    found[part].append(values[part])
            for part in range(3):
                spot = pl.ds(pl.multiple_of(part * 64 + block * 8, 8), 8)
                out[spot, :] = jnp.concatenate(found[part], 0)
            return carry

        lax.fori_loop(first, end, body, 0)

    def gather_ghosts(values):
        stacked = halves(values)

        def body(block, carry):
            found = [[], [], []]
            for step in range(8):
                spot = pl.ds(step * LANES, LANES)
                rows = joined(dot(stacked, lane_hots[block, :, spot]))
                ghost_hot = row_hots[block, GHOST_ROW:ROWS, spot]
                hang_hot = row_hots[block, HANG_ROW : HANG_ROW + 1, spot]
                hung = rows[24:32] * hang_hot
                for part in range(3):
                    total = jnp.sum(
                        rows[part * 8 : part * 8 + 8] * ghost_hot, axis=0, keepdims=True
                    )
                    found[part].append(total + hung[part : part + 1])
            for part in range(3):
                spot = pl.ds(pl.multiple_of(part * 64 + block * 8, 8), 8)
                cells[spot, :] = owned_cells[spot, :] + jnp.concatenate(found[part], 0)
            return carry

        lax.fori_loop(0, 8, body, 0)

    def image_rows(block):
        return [
            image[pl.ds(pl.multiple_of(part * 64 + block * 8, 8), 8), :] for part in range(3)
        ]

    def scatter_ghosts():
        def body(block, total):
            columns = []
            rows = image_rows(block)
            for step in range(8):
                spot = pl.ds(step * LANES, LANES)
                ghost_hot = row_hots[block, GHOST_ROW:ROWS, spot]
                hang_hot = row_hots[block, HANG_ROW : HANG_ROW + 1, spot]
                values = [each[step : step + 1] for each in rows]
                hung = jnp.concatenate(
                    [value * hang_hot for value in values] + [jnp.zeros((5, LANES), F32)], 0
                )
                columns.append(
                    halves(jnp.concatenate([value * ghost_hot for value in values] + [hung], 0))
                )
            return total + dot_nt(jnp.concatenate(columns, 1), lane_hots[block])

        return joined(lax.fori_loop(0, 8, body, jnp.zeros((64, LANES), F32)))

    def scatter_owned():
        def body(block, total):
            columns = []
            rows = image_rows(block)
            for step in range(8):
                spot = pl.ds(step * LANES, LANES)
                row_hot = row_hots[block, :GHOST_ROW, spot]
                columns.append(spread([each[step : step + 1] for each in rows], row_hot))
            return total + dot_nt(jnp.concatenate(columns, 1), lane_hots[block])

        return joined(lax.fori_loop(0, 8, body, jnp.zeros((6 * GHOST_ROW, LANES), F32)))

    def released(held, low, rows):
        columns = []
        for step in range(8):
            spot = pl.ds(step * LANES, LANES)
            columns.append(spread(held, master_rows[low : low + rows, spot]))
        return joined(dot_nt(jnp.concatenate(columns, 1), master_lanes[...]))

    def product(values, form):
        high = values.astype(BF16)
        low = (values - high.astype(F32)).astype(BF16)
        return form(stiff_high, high) + form(stiff_high, low) + form(stiff_low, high)

    owned_masters = masters(table[...], 0, GHOST_ROW)
    gather_rows(halves(table[...]), GHOST_ROW, owned_cells, 0, 8)
    for k in (1, 2, 6, 5):
        loads[k].wait()
    stiff = stiff_ref[...]
    stiff_high = stiff.astype(BF16)
    stiff_low = (stiff - stiff_high.astype(F32)).astype(BF16)
    modulus = modulus_ref[...]
    fill(source, GHOST_ROW, source_ref)
    fill(inverse, GHOST_ROW, inverse_ref)

    recv = recv_first
    for sweep in range(SWEEPS):
        finish(pending)
        values = imported(recv, 0)
        hung = hanging(owned_masters, masters(values, GHOST_ROW, 8))
        gather_ghosts(jnp.concatenate([values, hung], 0))
        image[...] = modulus * product(cells[...], dot_tn)
        totals = scatter_ghosts()
        held = [
            jnp.concatenate([totals[24 + part : 25 + part, :128]] * 2, 1) for part in range(3)
        ]
        totals = totals[:24] + released(held, GHOST_ROW, 8)
        send, recv = send_ghost.at[2 * sweep], recv_ghost.at[2 * sweep]
        for slot in range(SLOTS):
            for part in range(3):
                spot = part * SLOTS + slot
                send[slot, 2 * part : 2 * part + 1, :] = totals[spot : spot + 1, :128]
                send[slot, 2 * part + 1 : 2 * part + 2, :] = totals[spot : spot + 1, 128:]
        pending = exchange(send, recv, 2 * sweep + 1, -1)

        totals = scatter_owned() + released(held, 0, GHOST_ROW)
        if sweep == 0:
            values = imported(recv_first, 3)
            hung = hanging(
                masters(owned_of(primal_table), 0, GHOST_ROW), masters(values, GHOST_ROW, 8)
            )
            for part in range(3):
                row = part * ROWS
                primal_table[row + HANG_ROW : row + HANG_ROW + 1, :] = hung[part : part + 1]
                primal_table[row + GHOST_ROW : row + ROWS, :] = values[
                    part * SLOTS : (part + 1) * SLOTS
                ]
            primal_stack[...] = halves(primal_table[...])
            gather_rows(primal_stack[...], ROWS, primal_cells, 0, PRIMAL_FIRST)
        if sweep == SWEEPS - 1:
            primal_cells[...] = modulus * product(primal_cells[...], dot)
            for k in (12, 13, 14):
                loads[k].wait()
            for slot in range(SLOTS):
                spot = pl.ds(slot * 128, 128)
                sub_lanes[:, spot] = one_hot(sub_cell_ref[slot : slot + 1, :], LANES, BF16)
                sub_rows[:, spot] = one_hot(sub_face_ref[slot : slot + 1, :], 8, F32)
                owner_lanes[:, spot] = one_hot(sub_owner_ref[slot : slot + 1, :], LANES, BF16)
        finish(pending)
        columns = []
        for slot in range(SLOTS):
            block = arrived(slot, -1, recv[slot])
            rows = [
                jnp.concatenate(
                    [block[2 * part : 2 * part + 1], block[2 * part + 1 : 2 * part + 2]], 1
                )
                for part in range(3)
            ]
            columns.append(spread(rows, list_rows[:, pl.ds(slot * LANES, LANES)]))
        returned = joined(dot_nt(jnp.concatenate(columns, 1), list_lanes[...]))
        table[...] = table[...] + RELAXATION * inverse[...] * (
            source[...] - (totals + returned)
        )
        send, recv = send_ghost.at[2 * sweep + 1], recv_ghost.at[2 * sweep + 1]
        export(table[...], send, 3)
        pending = exchange(send, recv, 2 * sweep + 2, 1)

        owned_masters = masters(table[...], 0, GHOST_ROW)
        gather_rows(halves(table[...]), GHOST_ROW, owned_cells, 0, 8)
        if sweep == 0:
            gather_rows(primal_stack[...], ROWS, primal_cells, PRIMAL_FIRST, 8)

    for part in range(3):
        for row in range(OWNED):
            spot = part * GHOST_ROW + row
            adjoint_ref[part : part + 1, row * LANES : (row + 1) * LANES] = table[
                spot : spot + 1, :
            ]
    loads[4].wait()
    face = lax.broadcasted_iota(jnp.int32, (16, 192), 0)
    node_id = lax.broadcasted_iota(jnp.int32, (16, 192), 1) & 63
    first, second, third = node_id >> 4, (node_id >> 2) & 3, node_id & 3
    axis_index = jnp.where(face < 2, first, jnp.where(face < 4, second, third))
    on_face = jnp.logical_and(face < 6, axis_index == 3 * (face & 1))
    faces = jnp.where(on_face, 1.0, 0.0).astype(BF16)

    finish(pending)
    values = imported(recv, 0)
    hung = hanging(owned_masters, masters(values, GHOST_ROW, 8))
    gather_ghosts(jnp.concatenate([values, hung], 0))
    applied = primal_cells[...]
    work = applied * cells[...]
    work_high = work.astype(BF16)
    work_low = (work - work_high.astype(F32)).astype(BF16)
    flux = (dot(faces, work_high) + dot(faces, work_low))[:8]
    found = joined(dot(halves(flux), sub_lanes[...])) * sub_rows[...]
    found = jnp.sum(found, axis=0, keepdims=True)
    for slot in range(SLOTS):
        send_sub[slot] = found[:, slot * 128 : (slot + 1) * 128]
    pending = exchange(send_sub, recv_sub, 2 * SWEEPS + 1, 1)
    cell_term = jnp.sum(cells[...] * (load_ref[...] - applied), axis=0, keepdims=True)
    finish(pending)
    received = jnp.concatenate(
        [arrived(slot, 1, recv_sub[slot]) for slot in range(SLOTS)], 1
    )
    stacked = halves(jnp.broadcast_to(received, (8, SLOTS * 128)))
    face_term = dot_nt(stacked, owner_lanes[...])
    face_term = face_term[0:1] + face_term[8:9]
    indicator_ref[...] = (jnp.abs(cell_term) + jnp.abs(face_term)) * (1.0 / 16.0)
    for away, copy in sent:
        pl.when(exists(away))(copy.wait_send)


def local(
    adjoint_start,
    adjoint_source,
    inverse_diagonal,
    primal_field,
    cell_load,
    modulus,
    stiffness,
    connectivity,
    hang_node,
    hang_master,
    hang_weight,
    ghost_lists,
    subface_cell,
    subface_face,
    subface_owner,
):
    turns = 2 * SWEEPS + 2
    operands = (
        adjoint_start,
        adjoint_source,
        inverse_diagonal,
        primal_field,
        cell_load,
        modulus.reshape(1, LANES),
        stiffness,
        connectivity,
        hang_node.reshape(1, 128),
        hang_master,
        hang_weight,
        ghost_lists,
        subface_cell,
        subface_face,
        subface_owner,
    )
    vmem = pltpu.VMEM
    adjoint, indicator = pl.pallas_call(
        kernel,
        out_shape=(
            jax.ShapeDtypeStruct((3, NODES_DEV), F32),
            jax.ShapeDtypeStruct((1, LANES), F32),
        ),
        in_specs=[pl.BlockSpec(memory_space=pl.ANY)] * 15,
        out_specs=(pl.BlockSpec(memory_space=pltpu.VMEM),) * 2,
        scratch_shapes=[vmem(each.shape, each.dtype) for each in operands]
        + [
            vmem((3 * GHOST_ROW, LANES), F32),
            vmem((3 * ROWS, LANES), F32),
            vmem((3 * GHOST_ROW, LANES), F32),
            vmem((3 * GHOST_ROW, LANES), F32),
            vmem((3 * SLOTS, LANES), F32),
            vmem((8, ROWS, 8 * LANES), F32),
            vmem((8, LANES, 8 * LANES), BF16),
            vmem((GHOST_ROW, SLOTS * LANES), F32),
            vmem((LANES, SLOTS * LANES), BF16),
            vmem((ROWS, 16 * 128), F32),
            vmem((LANES, 16 * 128), BF16),
            vmem((8, SLOTS * 128), F32),
            vmem((LANES, SLOTS * 128), BF16),
            vmem((LANES, SLOTS * 128), BF16),
            vmem((192, LANES), F32),
            vmem((192, LANES), F32),
            vmem((192, LANES), F32),
            vmem((192, LANES), F32),
            vmem((6 * ROWS, LANES), BF16),
            vmem((SLOTS, 12, 128), F32),
            vmem((SLOTS, 12, 128), F32),
            vmem((2 * SWEEPS, SLOTS, 6, 128), F32),
            vmem((2 * SWEEPS, SLOTS, 6, 128), F32),
            vmem((SLOTS, 1, 128), F32),
            vmem((SLOTS, 1, 128), F32),
            pltpu.SemaphoreType.DMA((turns, SLOTS)),
            pltpu.SemaphoreType.DMA((turns, SLOTS)),
            pltpu.SemaphoreType.DMA((15,)),
        ],
        compiler_params=pltpu.CompilerParams(
            collective_id=0, has_side_effects=True, vmem_limit_bytes=56 * 1024 * 1024
        ),
    )(*operands)
    return adjoint, indicator.reshape(LANES)


def solution(mesh):
    wide, flat = P(None, "dom"), P("dom")
    placed = (wide,) * 5 + (flat, P(), wide, flat) + (wide,) * 6
    return jax.shard_map(
        local, mesh=mesh, in_specs=placed, out_specs=(wide, flat), check_vma=False
    )
```

```python
import jax
import jax.numpy as jnp
from jax import lax
from jax.experimental import pallas as pl
from jax.experimental.pallas import tpu as pltpu
from jax.sharding import PartitionSpec as P

MESH = pl.DeviceIdType.MESH
F32 = jnp.float32
BF16 = jnp.bfloat16

REACH = 4
SLOTS = 2 * REACH
SWEEPS = 2
NODES_DEV = 6912
EXT = 8960
PAD_CODE = 16368
RELAXATION = 0.7
BUILD_FIRST = 4
PRIMAL_CUTS = (0, 1, 3, 4)

LANES = 128
OWNED = NODES_DEV // LANES
HANG_ROW = OWNED
STRIDE = 64
GHOSTS = 2 * SLOTS
OFFSETS = [step + 1 for step in range(REACH)] + [-(step + 1) for step in range(REACH)]


def modulo(values, divisor):
    quotient = ((values.astype(F32) + 0.5) * (1.0 / divisor)).astype(jnp.int32)
    return values - quotient * divisor


def place(slots):
    row = slots >> 7
    return row + jnp.where(row >= OWNED, STRIDE - OWNED, 0), slots & 127


def one_hot(row, count, dtype, low=0):
    spots = lax.broadcasted_iota(jnp.int32, (count, row.shape[1]), 0) + low
    return jnp.where(spots == row, 1.0, 0.0).astype(dtype)


def halves(values):
    high = values.astype(BF16).astype(F32)
    return jnp.concatenate([high, values - high], 0).astype(BF16)


def dot(a, b):
    return jnp.dot(a, b, preferred_element_type=F32)


def dot_nt(a, b):
    return lax.dot_general(a, b, (((1,), (1,)), ((), ())), preferred_element_type=F32)


def dot_tn(a, b):
    return lax.dot_general(a, b, (((0,), (0,)), ((), ())), preferred_element_type=F32)


def joined(values):
    half = values.shape[0] // 2
    return values[:half] + values[half:]


def looked_up(rows_of, spots, parts, start=None):
    found = start or [[jnp.zeros((8, LANES), F32)] * parts for _ in spots]
    found = [list(each) for each in found]
    for each, (rows, lanes) in zip(found, spots):
        for number, row_of in rows_of:
            hit = rows == number
            for part in range(parts):
                table = jnp.broadcast_to(row_of(part), (8, LANES))
                value = jnp.take_along_axis(table, lanes, axis=1, mode="promise_in_bounds")
                each[part] = jnp.where(hit, value, each[part])
    return found


def spread(values, row_hot):
    return halves(jnp.concatenate([row_hot * value for value in values], 0))


def kernel(*refs):
    operands, outputs, refs = refs[:15], refs[15:17], refs[17:]
    staged, refs = refs[:15], refs[15:]
    (
        start_ref,
        source_ref,
        inverse_ref,
        primal_ref,
        load_ref,
        modulus_ref,
        stiff_ref,
        connect_ref,
        node_ref,
        master_ref,
        weight_ref,
        lists_ref,
        sub_cell_ref,
        sub_face_ref,
        sub_owner_ref,
    ) = staged
    adjoint_ref, indicator_ref = outputs
    (
        table,
        primal_table,
        source,
        inverse,
        row_hots,
        ghost_hots,
        hang_hots,
        lane_hots,
        cell_rows,
        cell_lanes,
        list_hots,
        list_lanes,
        master_hots,
        master_lanes,
        owner_lanes,
        owned_cells,
        cells,
        image,
        primal_cells,
        send_first,
        recv_first,
        send_ghost,
        recv_ghost,
        send_sub,
        recv_sub,
        send_sem,
        recv_sem,
        load_sem,
    ) = refs
    me = lax.axis_index("dom")
    count = lax.axis_size("dom")

    def exists(offset):
        other = me + offset
        return jnp.logical_and(other >= 0, other < count)

    barrier = pltpu.get_barrier_semaphore()
    for offset in OFFSETS:

        @pl.when(exists(offset))
        def _(offset=offset):
            pl.semaphore_signal(
                barrier, inc=1, device_id=(me + offset,), device_id_type=MESH
            )

    loads = [
        pltpu.make_async_copy(operands[k], staged[k], load_sem.at[k]) for k in range(15)
    ]
    for k in (11, 0, 3, 7, 8, 9, 10, 1, 2, 6, 5, 12, 13, 14, 4):
        loads[k].start()

    sent = []

    def exchange(send, recv, turn, direction):
        copies = []
        for slot, offset in enumerate(OFFSETS):
            away = direction * offset
            copy = pltpu.make_async_remote_copy(
                src_ref=send.at[slot],
                dst_ref=recv.at[slot],
                send_sem=send_sem.at[turn, slot],
                recv_sem=recv_sem.at[turn, slot],
                device_id=(me + away,),
                device_id_type=MESH,
            )
            pl.when(exists(away))(copy.start)
            copies.append((-away, copy))
            sent.append((away, copy))
        return copies

    def finish(copies):
        for away, copy in copies:
            pl.when(exists(away))(copy.wait_recv)

    for slot, offset in enumerate(OFFSETS):

        @pl.when(jnp.logical_not(exists(-offset)))
        def _(slot=slot):
            recv_first[slot] = jnp.zeros((12, LANES), F32)
            recv_sub[slot] = jnp.zeros((1, LANES), F32)
            for turn in range(SWEEPS):
                recv_ghost[2 * turn + 1, slot] = jnp.zeros((6, LANES), F32)

        @pl.when(jnp.logical_not(exists(offset)))
        def _(slot=slot):
            for turn in range(SWEEPS):
                recv_ghost[2 * turn, slot] = jnp.zeros((6, LANES), F32)

    def fill(ref, values):
        for part in range(3):
            low = part * STRIDE
            ref[low + OWNED - 6 : low + STRIDE, :] = jnp.zeros((STRIDE - OWNED + 6, LANES), F32)
            for row in range(OWNED):
                ref[low + row : low + row + 1, :] = values[
                    part : part + 1, row * LANES : (row + 1) * LANES
                ]

    def owned_rows(ref):
        def row_of(row):
            return lambda part: ref[part * STRIDE + row : part * STRIDE + row + 1, :]

        return [(row, row_of(row)) for row in range(OWNED)]

    def ghost_rows(recv, first=0):
        def row_of(row):
            spot = row % 2
            return lambda part: recv[
                row // 2, 2 * (first + part) + spot : 2 * (first + part) + spot + 1, :
            ]

        return [(STRIDE + row, row_of(row)) for row in range(GHOSTS)]

    lane_ids = lax.broadcasted_iota(jnp.int32, (SLOTS, 256), 1)
    loads[11].wait()
    lists = modulo(17 * lists_ref[...] + lane_ids, NODES_DEV)
    list_spots = [
        (lists[:, LANES * half : LANES * (half + 1)] >> 7, lists[:, LANES * half : LANES * (half + 1)] & 127)
        for half in range(2)
    ]
    loads[0].wait()
    fill(table, start_ref)

    def export(ref, send, first=0):
        found = looked_up(owned_rows(ref), list_spots, 3)
        for part in range(3):
            for half in range(2):
                spot = 2 * (first + part) + half
                for slot in range(SLOTS):
                    send[slot, spot : spot + 1, :] = found[half][part][slot : slot + 1]

    export(table, send_first)
    loads[3].wait()
    fill(primal_table, primal_ref)
    export(primal_table, send_first, 3)

    for k in (7, 8, 9, 10):
        loads[k].wait()
    node = node_ref[...]
    spots = modulo(13 * node, NODES_DEV)
    hang_row = jnp.where(node == PAD_CODE, -1, spots >> 7)
    numbers = (lax.broadcasted_iota(jnp.int32, (1, LANES), 1) + 1).astype(F32)
    source[: STRIDE, :] = dot_nt(
        (one_hot(hang_row, STRIDE, F32) * numbers).astype(BF16),
        one_hot(spots & 127, LANES, BF16),
    )

    def build(block, carry):
        span = pl.ds(pl.multiple_of(block * 8, 8), 8)
        codes = connect_ref[span, :]
        rows, lanes = place(modulo(17 * codes + 27 * lane_ids, EXT))
        pairs = [(rows[:, :LANES], lanes[:, :LANES]), (rows[:, LANES:], lanes[:, LANES:])]
        number = [each[0] for each in looked_up(owned_rows(source), pairs, 1)]
        number = jnp.concatenate(number, 1).astype(jnp.int32)
        rows = jnp.where(number > 0, HANG_ROW, rows)
        lanes = jnp.where(number > 0, number - 1, lanes)
        cell_rows[span, :] = rows
        cell_lanes[span, :] = lanes
        hang_hots[span, :] = jnp.where(rows == HANG_ROW, 1.0, 0.0)
        for step in range(8):
            spot = pl.ds(step * 256, 256)
            lane_hots[block, :, spot] = one_hot(lanes[step : step + 1], LANES, BF16)
            row_hots[block, :, spot] = one_hot(rows[step : step + 1], STRIDE, BF16)
            ghost_hots[block, :, spot] = one_hot(rows[step : step + 1], GHOSTS, F32, STRIDE)
        return carry

    lax.fori_loop(0, BUILD_FIRST, build, 0)
    peers = jnp.minimum(me, REACH) + jnp.minimum(count - 1 - me, REACH)
    pl.semaphore_wait(barrier, peers)
    pending = exchange(send_first, recv_first, 0, 1)
    lax.fori_loop(BUILD_FIRST, 8, build, 0)

    hang_ids = lax.broadcasted_iota(jnp.int32, (16, LANES), 1)
    rows, lanes = place(modulo(17 * master_ref[...] + 8 * hang_ids, EXT))
    weight = weight_ref[...]
    master_spots = [(rows[:8], lanes[:8]), (rows[8:], lanes[8:])]
    for step in range(16):
        spot = pl.ds(step * LANES, LANES)
        master_lanes[:, spot] = one_hot(lanes[step : step + 1], LANES, BF16)
        master_hots[:, spot] = (
            one_hot(rows[step : step + 1], STRIDE + GHOSTS, F32) * weight[step : step + 1]
        )

    def hanging(found):
        rows = []
        for part in range(3):
            total = found[0][part] * weight[:8] + found[1][part] * weight[8:]
            rows.append(jnp.sum(total, axis=0, keepdims=True))
        return rows

    def hang_rows(values):
        return [(HANG_ROW, lambda part: values[part])]

    def gather_cells(rows_of, base, out, first, end):
        def body(group, carry):
            spots, spans = [], []
            for block in range(2):
                for half in range(2):
                    low = pl.multiple_of(group * 16 + block * 8, 8)
                    lane = pl.ds(half * LANES, LANES)
                    spots.append((cell_rows[pl.ds(low, 8), lane], cell_lanes[pl.ds(low, 8), lane]))
                    spans.append((low, lane))

            def span(part, where):
                return pl.ds(pl.multiple_of(part * 64 + where[0], 8), 8), where[1]

            start = None
            if base is not None:
                start = [[base[span(part, where)] for part in range(3)] for where in spans]
            found = looked_up(rows_of, spots, 3, start)
            for values, where in zip(found, spans):
                for part in range(3):
                    out[span(part, where)] = values[part]
            return carry

        lax.fori_loop(first, end, body, 0)

    def image_rows(block):
        return [
            image[pl.ds(pl.multiple_of(part * 64 + block * 8, 8), 8), :] for part in range(3)
        ]

    def scatter_ghosts():
        def body(block, total):
            columns = []
            rows = image_rows(block)
            hang_hot = hang_hots[pl.ds(pl.multiple_of(block * 8, 8), 8), :]
            hung = [each * hang_hot for each in rows]
            for step in range(8):
                spot = pl.ds(step * 256, 256)
                ghost_hot = ghost_hots[block, :, spot]
                columns.append(
                    halves(
                        jnp.concatenate(
                            [each[step : step + 1] * ghost_hot for each in rows]
                            + [each[step : step + 1] for each in hung]
                            + [jnp.zeros((5, 256), F32)],
                            0,
                        )
                    )
                )
            return total + dot_nt(jnp.concatenate(columns, 1), lane_hots[block])

        zero = jnp.zeros((2 * (3 * GHOSTS + 8), LANES), F32)
        return joined(lax.fori_loop(0, 8, body, zero))

    def scatter_owned():
        def body(block, total):
            columns = []
            rows = image_rows(block)
            high = [each.astype(BF16).astype(F32) for each in rows]
            values = high + [a - b for a, b in zip(rows, high)]
            for step in range(8):
                spot = pl.ds(step * 256, 256)
                row_hot = row_hots[block, :, spot]
                column = []
                for each in values:
                    tile = jnp.broadcast_to(each[step : step + 1], (16, 256)).astype(BF16)
                    column.append(row_hot * jnp.concatenate([tile] * (STRIDE // 16), 0))
                columns.append(jnp.concatenate(column, 0))
            return total + dot_nt(jnp.concatenate(columns, 1), lane_hots[block])

        return joined(lax.fori_loop(0, 8, body, jnp.zeros((6 * STRIDE, LANES), F32)))

    def released(held, low, rows):
        columns = []
        for step in range(8):
            spot = pl.ds(step * 256, 256)
            columns.append(spread(held, master_hots[low : low + rows, spot]))
        return joined(dot_nt(jnp.concatenate(columns, 1), master_lanes[...]))

    def product(values, form):
        high = values.astype(BF16)
        low = (values - high.astype(F32)).astype(BF16)
        return form(stiff_high, high) + form(stiff_high, low) + form(stiff_low, high)

    owned_masters = looked_up(owned_rows(table), master_spots, 3)
    gather_cells(owned_rows(table), None, owned_cells, 0, 4)
    for k in (1, 2, 6, 5):
        loads[k].wait()
    stiff = stiff_ref[...]
    stiff_high = stiff.astype(BF16)
    stiff_low = (stiff - stiff_high.astype(F32)).astype(BF16)
    modulus = modulus_ref[...]
    fill(source, source_ref)
    fill(inverse, inverse_ref)
    for slot in range(SLOTS):
        row = lists[slot : slot + 1]
        spot = pl.ds(slot * 256, 256)
        list_lanes[:, spot] = one_hot(row & 127, LANES, BF16)
        list_hots[:, spot] = one_hot(row >> 7, STRIDE, F32)

    recv, first = recv_first, 0
    for sweep in range(SWEEPS):
        finish(pending)
        hung = hanging(looked_up(ghost_rows(recv), master_spots, 3, owned_masters))
        gather_cells(ghost_rows(recv) + hang_rows(hung), owned_cells, cells, 0, 4)
        image[...] = modulus * product(cells[...], dot_tn)
        totals = scatter_ghosts()
        held = [
            jnp.concatenate([totals[3 * GHOSTS + part : 3 * GHOSTS + part + 1]] * 2, 1)
            for part in range(3)
        ]
        totals = totals[: 3 * GHOSTS] + released(held, STRIDE, GHOSTS)
        send, recv = send_ghost.at[2 * sweep], recv_ghost.at[2 * sweep]
        for slot in range(SLOTS):
            for part in range(3):
                spot = part * GHOSTS + 2 * slot
                send[slot, 2 * part : 2 * part + 2, :] = totals[spot : spot + 2]
        pending = exchange(send, recv, 2 * sweep + 1, -1)

        totals = scatter_owned() + released(held, 0, STRIDE)
        if sweep == 0:
            primal_rows = owned_rows(primal_table) + ghost_rows(recv_first, 3)
            primal_rows += hang_rows(hanging(looked_up(primal_rows, master_spots, 3)))
        if sweep == SWEEPS - 1:
            primal_cells[...] = modulus * product(primal_cells[...], dot)
            for k in (12, 13, 14):
                loads[k].wait()
            for slot in range(SLOTS):
                owner_lanes[:, pl.ds(slot * LANES, LANES)] = one_hot(
                    sub_owner_ref[slot : slot + 1, :], 256, BF16
                )
        else:
            gather_cells(
                primal_rows, None, primal_cells, PRIMAL_CUTS[2 * sweep], PRIMAL_CUTS[2 * sweep + 1]
            )
        finish(pending)
        columns = []
        for slot in range(SLOTS):
            rows = [
                jnp.concatenate(
                    [recv[slot, 2 * part : 2 * part + 1, :], recv[slot, 2 * part + 1 : 2 * part + 2, :]],
                    1,
                )
                for part in range(3)
            ]
            columns.append(spread(rows, list_hots[:, pl.ds(slot * 256, 256)]))
        returned = joined(dot_nt(jnp.concatenate(columns, 1), list_lanes[...]))
        table[...] = table[...] + RELAXATION * inverse[...] * (
            source[...] - (totals + returned)
        )
        send, recv = send_ghost.at[2 * sweep + 1], recv_ghost.at[2 * sweep + 1]
        export(table, send)
        pending = exchange(send, recv, 2 * sweep + 2, 1)

        owned_masters = looked_up(owned_rows(table), master_spots, 3)
        gather_cells(owned_rows(table), None, owned_cells, 0, 4)
        if sweep == 0:
            gather_cells(primal_rows, None, primal_cells, PRIMAL_CUTS[1], 4)

    for part in range(3):
        for row in range(OWNED):
            spot = part * STRIDE + row
            adjoint_ref[part : part + 1, row * LANES : (row + 1) * LANES] = table[
                spot : spot + 1, :
            ]
    loads[4].wait()
    face = lax.broadcasted_iota(jnp.int32, (16, 192), 0)
    node_id = lax.broadcasted_iota(jnp.int32, (16, 192), 1) & 63
    first, second, third = node_id >> 4, (node_id >> 2) & 3, node_id & 3
    axis_index = jnp.where(face < 2, first, jnp.where(face < 4, second, third))
    on_face = jnp.logical_and(face < 6, axis_index == 3 * (face & 1))
    faces = jnp.where(on_face, 1.0, 0.0).astype(BF16)
    sub_cell = sub_cell_ref[...]
    sub_spot = (2 * sub_face_ref[...] + (sub_cell >> 7), sub_cell & 127)

    finish(pending)
    hung = hanging(looked_up(ghost_rows(recv), master_spots, 3, owned_masters))
    gather_cells(ghost_rows(recv) + hang_rows(hung), owned_cells, cells, 0, 4)
    applied = primal_cells[...]
    work = applied * cells[...]
    work_high = work.astype(BF16)
    work_low = (work - work_high.astype(F32)).astype(BF16)
    flux = dot(faces, work_high) + dot(faces, work_low)

    def flux_row(face, half):
        return lambda part: flux[face : face + 1, half * LANES : (half + 1) * LANES]

    flux_rows = [(2 * face + half, flux_row(face, half)) for face in range(6) for half in range(2)]
    found = looked_up(flux_rows, [sub_spot], 1)[0][0]
    for slot in range(SLOTS):
        send_sub[slot] = found[slot : slot + 1]
    pending = exchange(send_sub, recv_sub, 2 * SWEEPS + 1, 1)
    cell_term = jnp.sum(cells[...] * (load_ref[...] - applied), axis=0, keepdims=True)
    finish(pending)
    received = jnp.concatenate([recv_sub[slot] for slot in range(SLOTS)], 1)
    stacked = halves(jnp.broadcast_to(received, (8, SLOTS * LANES)))
    face_term = dot_nt(stacked, owner_lanes[...])
    face_term = face_term[0:1] + face_term[8:9]
    indicator_ref[...] = (jnp.abs(cell_term) + jnp.abs(face_term)) * (1.0 / 16.0)
    for away, copy in sent:
        pl.when(exists(away))(copy.wait_send)


def local(
    adjoint_start,
    adjoint_source,
    inverse_diagonal,
    primal_field,
    cell_load,
    modulus,
    stiffness,
    connectivity,
    hang_node,
    hang_master,
    hang_weight,
    ghost_lists,
    subface_cell,
    subface_face,
    subface_owner,
):
    turns = 2 * SWEEPS + 2
    operands = (
        adjoint_start,
        adjoint_source,
        inverse_diagonal,
        primal_field,
        cell_load,
        modulus.reshape(1, 256),
        stiffness,
        connectivity,
        hang_node.reshape(1, 128),
        hang_master,
        hang_weight,
        ghost_lists,
        subface_cell,
        subface_face,
        subface_owner,
    )
    vmem = pltpu.VMEM
    adjoint, indicator = pl.pallas_call(
        kernel,
        out_shape=(
            jax.ShapeDtypeStruct((3, NODES_DEV), F32),
            jax.ShapeDtypeStruct((1, 256), F32),
        ),
        in_specs=[pl.BlockSpec(memory_space=pl.ANY)] * 15,
        out_specs=(pl.BlockSpec(memory_space=pltpu.VMEM),) * 2,
        scratch_shapes=[vmem(each.shape, each.dtype) for each in operands]
        + [
            vmem((3 * STRIDE, LANES), F32),
            vmem((3 * STRIDE, LANES), F32),
            vmem((3 * STRIDE, LANES), F32),
            vmem((3 * STRIDE, LANES), F32),
            vmem((8, STRIDE, 8 * 256), BF16),
            vmem((8, GHOSTS, 8 * 256), F32),
            vmem((64, 256), F32),
            vmem((8, LANES, 8 * 256), BF16),
            vmem((64, 256), jnp.int32),
            vmem((64, 256), jnp.int32),
            vmem((STRIDE, SLOTS * 256), F32),
            vmem((LANES, SLOTS * 256), BF16),
            vmem((STRIDE + GHOSTS, 16 * LANES), F32),
            vmem((LANES, 16 * LANES), BF16),
            vmem((256, SLOTS * LANES), BF16),
            vmem((192, 256), F32),
            vmem((192, 256), F32),
            vmem((192, 256), F32),
            vmem((192, 256), F32),
            vmem((SLOTS, 12, LANES), F32),
            vmem((SLOTS, 12, LANES), F32),
            vmem((2 * SWEEPS, SLOTS, 6, LANES), F32),
            vmem((2 * SWEEPS, SLOTS, 6, LANES), F32),
            vmem((SLOTS, 1, LANES), F32),
            vmem((SLOTS, 1, LANES), F32),
            pltpu.SemaphoreType.DMA((turns, SLOTS)),
            pltpu.SemaphoreType.DMA((turns, SLOTS)),
            pltpu.SemaphoreType.DMA((15,)),
        ],
        compiler_params=pltpu.CompilerParams(
            collective_id=0, has_side_effects=True, vmem_limit_bytes=56 * 1024 * 1024
        ),
    )(*operands)
    return adjoint, indicator.reshape(256)


def solution(mesh):
    wide, flat = P(None, "dom"), P("dom")
    placed = (wide,) * 5 + (flat, P(), wide, flat) + (wide,) * 6
    return jax.shard_map(
        local, mesh=mesh, in_specs=placed, out_specs=(wide, flat), check_vma=False
    )
```

```python
import functools

import jax
import jax.numpy as jnp
from jax import lax
from jax.experimental import pallas as pl
from jax.experimental.pallas import tpu as pltpu
from jax.sharding import PartitionSpec as P

MESH = pl.DeviceIdType.MESH
F32 = jnp.float32
BF16 = jnp.bfloat16

REACH = 4
SLOTS = 2 * REACH
SWEEPS = 2
NODES_DEV = 6912
EXT = 8960
PAD_CODE = 16368
RELAXATION = 0.7
BUILD_FIRST = 2

LANES = 128
OWNED = NODES_DEV // LANES
HANG_ROW = OWNED
STRIDE = 64
GHOSTS = 2 * SLOTS
OFFSETS = [step + 1 for step in range(REACH)] + [-(step + 1) for step in range(REACH)]


def modulo(values, divisor):
    quotient = ((values.astype(F32) + 0.5) * (1.0 / divisor)).astype(jnp.int32)
    return values - quotient * divisor


def place(slots):
    row = slots >> 7
    return row + jnp.where(row >= OWNED, STRIDE - OWNED, 0), slots & 127


def one_hot(row, count, dtype, low=0):
    spots = lax.broadcasted_iota(jnp.int32, (count, row.shape[1]), 0) + low
    return jnp.where(spots == row, 1.0, 0.0).astype(dtype)


def halves(values):
    high = values.astype(BF16).astype(F32)
    return jnp.concatenate([high, values - high], 0).astype(BF16)


def dot(a, b):
    return jnp.dot(a, b, preferred_element_type=F32)


def dot_nt(a, b):
    return lax.dot_general(a, b, (((1,), (1,)), ((), ())), preferred_element_type=F32)


def dot_tn(a, b):
    return lax.dot_general(a, b, (((0,), (0,)), ((), ())), preferred_element_type=F32)


def joined(values):
    half = values.shape[0] // 2
    return values[:half] + values[half:]


def looked_up(rows_of, spots, parts, start=None):
    found = start or [[jnp.zeros((8, LANES), F32)] * parts for _ in spots]
    found = [list(each) for each in found]
    for each, (rows, lanes) in zip(found, spots):
        for number, row_of in rows_of:
            hit = rows == number
            for part in range(parts):
                table = jnp.broadcast_to(row_of(part), (8, LANES))
                value = jnp.take_along_axis(table, lanes, axis=1, mode="promise_in_bounds")
                each[part] = jnp.where(hit, value, each[part])
    return found


def spread(values, row_hot):
    return halves(jnp.concatenate([row_hot * value for value in values], 0))


def kernel(*refs):
    operands, outputs, refs = refs[:15], refs[15:17], refs[17:]
    staged, refs = refs[:15], refs[15:]
    (
        start_ref,
        source_ref,
        inverse_ref,
        primal_ref,
        load_ref,
        modulus_ref,
        stiff_ref,
        connect_ref,
        node_ref,
        master_ref,
        weight_ref,
        lists_ref,
        sub_cell_ref,
        sub_face_ref,
        sub_owner_ref,
    ) = staged
    adjoint_ref, indicator_ref = outputs
    (
        table,
        primal_table,
        source,
        inverse,
        row_hots,
        ghost_hots,
        hang_hots,
        lane_hots,
        cell_rows,
        cell_lanes,
        list_hots,
        list_lanes,
        master_hots,
        master_lanes,
        owner_lanes,
        owned_cells,
        cells,
        image,
        primal_cells,
        send_first,
        recv_first,
        send_ghost,
        recv_ghost,
        send_sub,
        recv_sub,
        send_sem,
        recv_sem,
        load_sem,
    ) = refs
    me = lax.axis_index("dom")
    count = lax.axis_size("dom")

    def exists(offset):
        other = me + offset
        return jnp.logical_and(other >= 0, other < count)

    barrier = pltpu.get_barrier_semaphore()
    for offset in OFFSETS:

        @pl.when(exists(offset))
        def _(offset=offset):
            pl.semaphore_signal(
                barrier, inc=1, device_id=(me + offset,), device_id_type=MESH
            )

    loads = [
        pltpu.make_async_copy(operands[k], staged[k], load_sem.at[k]) for k in range(15)
    ]
    for k in (11, 0, 3, 7, 8, 9, 10, 1, 2, 6, 5, 12, 13, 14, 4):
        loads[k].start()

    sent = []

    def exchange(send, recv, turn, direction):
        copies = []
        for slot, offset in enumerate(OFFSETS):
            away = direction * offset
            copy = pltpu.make_async_remote_copy(
                src_ref=send.at[slot],
                dst_ref=recv.at[slot],
                send_sem=send_sem.at[turn, slot],
                recv_sem=recv_sem.at[turn, slot],
                device_id=(me + away,),
                device_id_type=MESH,
            )
            pl.when(exists(away))(copy.start)
            copies.append((-away, copy))
            sent.append((away, copy))
        return copies

    def finish(copies):
        for away, copy in copies:
            pl.when(exists(away))(copy.wait_recv)

    for slot, offset in enumerate(OFFSETS):

        @pl.when(jnp.logical_not(exists(-offset)))
        def _(slot=slot):
            recv_first[slot] = jnp.zeros((12, LANES), F32)
            recv_sub[slot] = jnp.zeros((1, LANES), F32)
            for turn in range(SWEEPS):
                recv_ghost[2 * turn + 1, slot] = jnp.zeros((6, LANES), F32)

        @pl.when(jnp.logical_not(exists(offset)))
        def _(slot=slot):
            for turn in range(SWEEPS):
                recv_ghost[2 * turn, slot] = jnp.zeros((6, LANES), F32)

    def fill(ref, values):
        for part in range(3):
            low = part * STRIDE
            ref[low + OWNED - 6 : low + STRIDE, :] = jnp.zeros((STRIDE - OWNED + 6, LANES), F32)
            for row in range(OWNED):
                ref[low + row : low + row + 1, :] = values[
                    part : part + 1, row * LANES : (row + 1) * LANES
                ]

    def owned_rows(ref):
        def row_of(row):
            return lambda part: ref[part * STRIDE + row : part * STRIDE + row + 1, :]

        return [(row, row_of(row)) for row in range(OWNED)]

    def ghost_rows(recv, first=0):
        def row_of(row):
            spot = row % 2
            return lambda part: recv[
                row // 2, 2 * (first + part) + spot : 2 * (first + part) + spot + 1, :
            ]

        return [(STRIDE + row, row_of(row)) for row in range(GHOSTS)]

    lane_ids = lax.broadcasted_iota(jnp.int32, (SLOTS, 256), 1)
    loads[11].wait()
    lists = modulo(17 * lists_ref[...] + lane_ids, NODES_DEV)
    list_spots = [
        (lists[:, LANES * half : LANES * (half + 1)] >> 7, lists[:, LANES * half : LANES * (half + 1)] & 127)
        for half in range(2)
    ]
    loads[0].wait()
    fill(table, start_ref)

    def export(ref, send, first=0):
        found = looked_up(owned_rows(ref), list_spots, 3)
        for part in range(3):
            for half in range(2):
                spot = 2 * (first + part) + half
                for slot in range(SLOTS):
                    send[slot, spot : spot + 1, :] = found[half][part][slot : slot + 1]

    export(table, send_first)
    loads[3].wait()
    fill(primal_table, primal_ref)
    export(primal_table, send_first, 3)

    for k in (7, 8, 9, 10):
        loads[k].wait()
    node = node_ref[...]
    spots = modulo(13 * node, NODES_DEV)
    hang_row = jnp.where(node == PAD_CODE, -1, spots >> 7)
    numbers = (lax.broadcasted_iota(jnp.int32, (1, LANES), 1) + 1).astype(F32)
    source[: STRIDE, :] = dot_nt(
        (one_hot(hang_row, STRIDE, F32) * numbers).astype(BF16),
        one_hot(spots & 127, LANES, BF16),
    )

    def build(block, carry):
        span = pl.ds(pl.multiple_of(block * 8, 8), 8)
        codes = connect_ref[span, :]
        rows, lanes = place(modulo(17 * codes + 27 * lane_ids, EXT))
        pairs = [(rows[:, :LANES], lanes[:, :LANES]), (rows[:, LANES:], lanes[:, LANES:])]
        number = [each[0] for each in looked_up(owned_rows(source), pairs, 1)]
        number = jnp.concatenate(number, 1).astype(jnp.int32)
        rows = jnp.where(number > 0, HANG_ROW, rows)
        lanes = jnp.where(number > 0, number - 1, lanes)
        cell_rows[span, :] = rows
        cell_lanes[span, :] = lanes
        hang_hots[span, :] = jnp.where(rows == HANG_ROW, 1.0, 0.0)
        return carry

    lax.fori_loop(0, 8, build, 0)

    def build_hots(block):
        span = pl.ds(pl.multiple_of(block * 8, 8), 8)
        rows, lanes = cell_rows[span, :], cell_lanes[span, :]
        for step in range(8):
            spot = pl.ds(step * 256, 256)
            lane_hots[block, :, spot] = one_hot(lanes[step : step + 1], LANES, BF16)
            row_hots[block, :, spot] = one_hot(rows[step : step + 1], STRIDE, BF16)
            ghost_hots[block, :, spot] = one_hot(rows[step : step + 1], GHOSTS, F32, STRIDE)

    def gather_block(rows_of, base, out, block, blocks=1):
        spots, spans = [], []
        for step in range(blocks):
            low = pl.multiple_of((block * blocks + step) * 8, 8)
            for half in range(2):
                lane = pl.ds(half * LANES, LANES)
                spots.append((cell_rows[pl.ds(low, 8), lane], cell_lanes[pl.ds(low, 8), lane]))
                spans.append((low, lane))

        def span(part, where):
            return pl.ds(pl.multiple_of(part * 64 + where[0], 8), 8), where[1]

        start = None
        if base is not None:
            start = [[base[span(part, where)] for part in range(3)] for where in spans]
        found = looked_up(rows_of, spots, 3, start)
        for values, where in zip(found, spans):
            for part in range(3):
                out[span(part, where)] = values[part]

    def build_and_gather(block, carry):
        build_hots(block)
        gather_block(owned_rows(table), None, owned_cells, block)
        return carry

    lax.fori_loop(0, BUILD_FIRST, build_and_gather, 0)
    peers = jnp.minimum(me, REACH) + jnp.minimum(count - 1 - me, REACH)
    pl.semaphore_wait(barrier, peers)
    pending = exchange(send_first, recv_first, 0, 1)
    lax.fori_loop(BUILD_FIRST, 8, build_and_gather, 0)

    hang_ids = lax.broadcasted_iota(jnp.int32, (16, LANES), 1)
    rows, lanes = place(modulo(17 * master_ref[...] + 8 * hang_ids, EXT))
    weight = weight_ref[...]
    master_spots = [(rows[:8], lanes[:8]), (rows[8:], lanes[8:])]
    for step in range(16):
        spot = pl.ds(step * LANES, LANES)
        master_lanes[:, spot] = one_hot(lanes[step : step + 1], LANES, BF16)
        master_hots[:, spot] = (
            one_hot(rows[step : step + 1], STRIDE + GHOSTS, F32) * weight[step : step + 1]
        )

    def hanging(found):
        rows = []
        for part in range(3):
            total = found[0][part] * weight[:8] + found[1][part] * weight[8:]
            rows.append(jnp.sum(total, axis=0, keepdims=True))
        return rows

    def hang_rows(values):
        return [(HANG_ROW, lambda part: values[part])]

    def gather_cells(rows_of, base, out, blocks):
        def body(group, carry):
            gather_block(rows_of, base, out, group, blocks)
            return carry

        lax.fori_loop(0, 8 // blocks, body, 0)

    def image_rows(block):
        return [
            image[pl.ds(pl.multiple_of(part * 64 + block * 8, 8), 8), :] for part in range(3)
        ]

    def scatter_ghosts():
        def body(block, total):
            columns = []
            rows = image_rows(block)
            hang_hot = hang_hots[pl.ds(pl.multiple_of(block * 8, 8), 8), :]
            hung = [each * hang_hot for each in rows]
            for step in range(8):
                spot = pl.ds(step * 256, 256)
                ghost_hot = ghost_hots[block, :, spot]
                columns.append(
                    halves(
                        jnp.concatenate(
                            [each[step : step + 1] * ghost_hot for each in rows]
                            + [each[step : step + 1] for each in hung]
                            + [jnp.zeros((5, 256), F32)],
                            0,
                        )
                    )
                )
            return total + dot_nt(jnp.concatenate(columns, 1), lane_hots[block])

        zero = jnp.zeros((2 * (3 * GHOSTS + 8), LANES), F32)
        return joined(lax.fori_loop(0, 8, body, zero))

    def scatter_owned(beside=None):
        def body(block, total):
            if beside is not None:
                beside(block)
            columns = []
            rows = image_rows(block)
            high = [each.astype(BF16).astype(F32) for each in rows]
            values = high + [a - b for a, b in zip(rows, high)]
            for step in range(8):
                spot = pl.ds(step * 256, 256)
                row_hot = row_hots[block, :, spot]
                column = []
                for each in values:
                    tile = jnp.broadcast_to(each[step : step + 1], (16, 256)).astype(BF16)
                    column.append(row_hot * jnp.concatenate([tile] * (STRIDE // 16), 0))
                columns.append(jnp.concatenate(column, 0))
            return total + dot_nt(jnp.concatenate(columns, 1), lane_hots[block])

        return joined(lax.fori_loop(0, 8, body, jnp.zeros((6 * STRIDE, LANES), F32)))

    def released(held, low, rows):
        columns = []
        for step in range(8):
            spot = pl.ds(step * 256, 256)
            columns.append(spread(held, master_hots[low : low + rows, spot]))
        return joined(dot_nt(jnp.concatenate(columns, 1), master_lanes[...]))

    def product(values, form):
        high = values.astype(BF16)
        low = (values - high.astype(F32)).astype(BF16)
        return form(stiff_high, high) + form(stiff_high, low) + form(stiff_low, high)

    owned_masters = looked_up(owned_rows(table), master_spots, 3)
    for k in (1, 2, 6, 5):
        loads[k].wait()
    stiff = stiff_ref[...]
    stiff_high = stiff.astype(BF16)
    stiff_low = (stiff - stiff_high.astype(F32)).astype(BF16)
    modulus = modulus_ref[...]
    fill(source, source_ref)
    fill(inverse, inverse_ref)
    for slot in range(SLOTS):
        row = lists[slot : slot + 1]
        spot = pl.ds(slot * 256, 256)
        list_lanes[:, spot] = one_hot(row & 127, LANES, BF16)
        list_hots[:, spot] = one_hot(row >> 7, STRIDE, F32)

    recv, first = recv_first, 0
    for sweep in range(SWEEPS):
        finish(pending)
        hung = hanging(looked_up(ghost_rows(recv), master_spots, 3, owned_masters))
        gather_cells(ghost_rows(recv) + hang_rows(hung), owned_cells, cells, 4)
        image[...] = modulus * product(cells[...], dot_tn)
        totals = scatter_ghosts()
        held = [
            jnp.concatenate([totals[3 * GHOSTS + part : 3 * GHOSTS + part + 1]] * 2, 1)
            for part in range(3)
        ]
        totals = totals[: 3 * GHOSTS] + released(held, STRIDE, GHOSTS)
        send, recv = send_ghost.at[2 * sweep], recv_ghost.at[2 * sweep]
        for slot in range(SLOTS):
            for part in range(3):
                spot = part * GHOSTS + 2 * slot
                send[slot, 2 * part : 2 * part + 2, :] = totals[spot : spot + 2]
        pending = exchange(send, recv, 2 * sweep + 1, -1)

        beside = None
        if sweep == 0:
            primal_rows = owned_rows(primal_table) + ghost_rows(recv_first, 3)
            primal_rows += hang_rows(hanging(looked_up(primal_rows, master_spots, 3)))
            beside = functools.partial(gather_block, primal_rows, None, primal_cells)
        totals = scatter_owned(beside) + released(held, 0, STRIDE)
        if sweep == SWEEPS - 1:
            primal_cells[...] = modulus * product(primal_cells[...], dot)
            for k in (12, 13, 14):
                loads[k].wait()
            for slot in range(SLOTS):
                owner_lanes[:, pl.ds(slot * LANES, LANES)] = one_hot(
                    sub_owner_ref[slot : slot + 1, :], 256, BF16
                )
        finish(pending)
        columns = []
        for slot in range(SLOTS):
            rows = [
                jnp.concatenate(
                    [recv[slot, 2 * part : 2 * part + 1, :], recv[slot, 2 * part + 1 : 2 * part + 2, :]],
                    1,
                )
                for part in range(3)
            ]
            columns.append(spread(rows, list_hots[:, pl.ds(slot * 256, 256)]))
        returned = joined(dot_nt(jnp.concatenate(columns, 1), list_lanes[...]))
        table[...] = table[...] + RELAXATION * inverse[...] * (
            source[...] - (totals + returned)
        )
        send, recv = send_ghost.at[2 * sweep + 1], recv_ghost.at[2 * sweep + 1]
        export(table, send)
        pending = exchange(send, recv, 2 * sweep + 2, 1)

        owned_masters = looked_up(owned_rows(table), master_spots, 3)
        gather_cells(owned_rows(table), None, owned_cells, 2)

    for part in range(3):
        for row in range(OWNED):
            spot = part * STRIDE + row
            adjoint_ref[part : part + 1, row * LANES : (row + 1) * LANES] = table[
                spot : spot + 1, :
            ]
    loads[4].wait()
    face = lax.broadcasted_iota(jnp.int32, (16, 192), 0)
    node_id = lax.broadcasted_iota(jnp.int32, (16, 192), 1) & 63
    first, second, third = node_id >> 4, (node_id >> 2) & 3, node_id & 3
    axis_index = jnp.where(face < 2, first, jnp.where(face < 4, second, third))
    on_face = jnp.logical_and(face < 6, axis_index == 3 * (face & 1))
    faces = jnp.where(on_face, 1.0, 0.0).astype(BF16)
    sub_cell = sub_cell_ref[...]
    sub_spot = (2 * sub_face_ref[...] + (sub_cell >> 7), sub_cell & 127)

    finish(pending)
    hung = hanging(looked_up(ghost_rows(recv), master_spots, 3, owned_masters))
    gather_cells(ghost_rows(recv) + hang_rows(hung), owned_cells, cells, 4)
    applied = primal_cells[...]
    work = applied * cells[...]
    work_high = work.astype(BF16)
    work_low = (work - work_high.astype(F32)).astype(BF16)
    flux = dot(faces, work_high) + dot(faces, work_low)

    def flux_row(face, half):
        return lambda part: flux[face : face + 1, half * LANES : (half + 1) * LANES]

    flux_rows = [(2 * face + half, flux_row(face, half)) for face in range(6) for half in range(2)]
    found = looked_up(flux_rows, [sub_spot], 1)[0][0]
    for slot in range(SLOTS):
        send_sub[slot] = found[slot : slot + 1]
    pending = exchange(send_sub, recv_sub, 2 * SWEEPS + 1, 1)
    cell_term = jnp.sum(cells[...] * (load_ref[...] - applied), axis=0, keepdims=True)
    finish(pending)
    received = jnp.concatenate([recv_sub[slot] for slot in range(SLOTS)], 1)
    stacked = halves(jnp.broadcast_to(received, (8, SLOTS * LANES)))
    face_term = dot_nt(stacked, owner_lanes[...])
    face_term = face_term[0:1] + face_term[8:9]
    indicator_ref[...] = (jnp.abs(cell_term) + jnp.abs(face_term)) * (1.0 / 16.0)
    for away, copy in sent:
        pl.when(exists(away))(copy.wait_send)


def local(
    adjoint_start,
    adjoint_source,
    inverse_diagonal,
    primal_field,
    cell_load,
    modulus,
    stiffness,
    connectivity,
    hang_node,
    hang_master,
    hang_weight,
    ghost_lists,
    subface_cell,
    subface_face,
    subface_owner,
):
    turns = 2 * SWEEPS + 2
    operands = (
        adjoint_start,
        adjoint_source,
        inverse_diagonal,
        primal_field,
        cell_load,
        modulus.reshape(1, 256),
        stiffness,
        connectivity,
        hang_node.reshape(1, 128),
        hang_master,
        hang_weight,
        ghost_lists,
        subface_cell,
        subface_face,
        subface_owner,
    )
    vmem = pltpu.VMEM
    adjoint, indicator = pl.pallas_call(
        kernel,
        out_shape=(
            jax.ShapeDtypeStruct((3, NODES_DEV), F32),
            jax.ShapeDtypeStruct((1, 256), F32),
        ),
        in_specs=[pl.BlockSpec(memory_space=pl.ANY)] * 15,
        out_specs=(pl.BlockSpec(memory_space=pltpu.VMEM),) * 2,
        scratch_shapes=[vmem(each.shape, each.dtype) for each in operands]
        + [
            vmem((3 * STRIDE, LANES), F32),
            vmem((3 * STRIDE, LANES), F32),
            vmem((3 * STRIDE, LANES), F32),
            vmem((3 * STRIDE, LANES), F32),
            vmem((8, STRIDE, 8 * 256), BF16),
            vmem((8, GHOSTS, 8 * 256), F32),
            vmem((64, 256), F32),
            vmem((8, LANES, 8 * 256), BF16),
            vmem((64, 256), jnp.int32),
            vmem((64, 256), jnp.int32),
            vmem((STRIDE, SLOTS * 256), F32),
            vmem((LANES, SLOTS * 256), BF16),
            vmem((STRIDE + GHOSTS, 16 * LANES), F32),
            vmem((LANES, 16 * LANES), BF16),
            vmem((256, SLOTS * LANES), BF16),
            vmem((192, 256), F32),
            vmem((192, 256), F32),
            vmem((192, 256), F32),
            vmem((192, 256), F32),
            vmem((SLOTS, 12, LANES), F32),
            vmem((SLOTS, 12, LANES), F32),
            vmem((2 * SWEEPS, SLOTS, 6, LANES), F32),
            vmem((2 * SWEEPS, SLOTS, 6, LANES), F32),
            vmem((SLOTS, 1, LANES), F32),
            vmem((SLOTS, 1, LANES), F32),
            pltpu.SemaphoreType.DMA((turns, SLOTS)),
            pltpu.SemaphoreType.DMA((turns, SLOTS)),
            pltpu.SemaphoreType.DMA((15,)),
        ],
        compiler_params=pltpu.CompilerParams(
            collective_id=0, has_side_effects=True, vmem_limit_bytes=56 * 1024 * 1024
        ),
    )(*operands)
    return adjoint, indicator.reshape(256)


def solution(mesh):
    wide, flat = P(None, "dom"), P("dom")
    placed = (wide,) * 5 + (flat, P(), wide, flat) + (wide,) * 6
    return jax.shard_map(
        local, mesh=mesh, in_specs=placed, out_specs=(wide, flat), check_vma=False
    )
```

```python
import functools

import jax
import jax.numpy as jnp
from jax import lax
from jax.experimental import pallas as pl
from jax.experimental.pallas import tpu as pltpu
from jax.sharding import PartitionSpec as P

MESH = pl.DeviceIdType.MESH
F32 = jnp.float32
BF16 = jnp.bfloat16

REACH = 4
SLOTS = 2 * REACH
SWEEPS = 2
NODES_DEV = 6912
EXT = 8960
PAD_CODE = 16368
RELAXATION = 0.7
BUILD_FIRST = 0

LANES = 128
OWNED = NODES_DEV // LANES
HANG_ROW = OWNED
STRIDE = 64
GHOSTS = 2 * SLOTS
OFFSETS = [step + 1 for step in range(REACH)] + [-(step + 1) for step in range(REACH)]
FAR_FIRST = sorted(range(SLOTS), key=lambda slot: -abs(OFFSETS[slot]))


def modulo(values, divisor):
    quotient = ((values.astype(F32) + 0.5) * (1.0 / divisor)).astype(jnp.int32)
    return values - quotient * divisor


def place(slots):
    row = slots >> 7
    return row + jnp.where(row >= OWNED, STRIDE - OWNED, 0), slots & 127


def one_hot(row, count, dtype, low=0):
    spots = lax.broadcasted_iota(jnp.int32, (count, row.shape[1]), 0) + low
    return jnp.where(spots == row, 1.0, 0.0).astype(dtype)


def halves(values):
    high = values.astype(BF16).astype(F32)
    return jnp.concatenate([high, values - high], 0).astype(BF16)


def dot(a, b):
    return jnp.dot(a, b, preferred_element_type=F32)


def dot_nt(a, b):
    return lax.dot_general(a, b, (((1,), (1,)), ((), ())), preferred_element_type=F32)


def dot_tn(a, b):
    return lax.dot_general(a, b, (((0,), (0,)), ((), ())), preferred_element_type=F32)


def joined(values):
    half = values.shape[0] // 2
    return values[:half] + values[half:]


def looked_up(rows_of, spots, parts, start=None):
    found = start or [[jnp.zeros((8, LANES), F32)] * parts for _ in spots]
    found = [list(each) for each in found]
    for each, (rows, lanes) in zip(found, spots):
        for number, row_of in rows_of:
            hit = rows == number
            for part in range(parts):
                table = jnp.broadcast_to(row_of(part), (8, LANES))
                value = jnp.take_along_axis(table, lanes, axis=1, mode="promise_in_bounds")
                each[part] = jnp.where(hit, value, each[part])
    return found


def split_rows(rows):
    high = [each.astype(BF16).astype(F32) for each in rows]
    return high + [a - b for a, b in zip(rows, high)]


def spread_whole(values, row_hot):
    column = []
    for each in values:
        tile = jnp.broadcast_to(each, (16, each.shape[1])).astype(BF16)
        column.append(row_hot * jnp.concatenate([tile] * (STRIDE // 16), 0))
    return jnp.concatenate(column, 0)


def spread(values, row_hot):
    return halves(jnp.concatenate([row_hot * value for value in values], 0))


def kernel(*refs):
    operands, outputs, refs = refs[:15], refs[15:17], refs[17:]
    staged, refs = refs[:15], refs[15:]
    (
        start_ref,
        source_ref,
        inverse_ref,
        primal_ref,
        load_ref,
        modulus_ref,
        stiff_ref,
        connect_ref,
        node_ref,
        master_ref,
        weight_ref,
        lists_ref,
        sub_cell_ref,
        sub_face_ref,
        sub_owner_ref,
    ) = staged
    adjoint_ref, indicator_ref = outputs
    (
        table,
        primal_table,
        source,
        inverse,
        row_hots,
        ghost_hots,
        hang_hots,
        lane_hots,
        cell_rows,
        cell_lanes,
        list_hots,
        list_lanes,
        master_hots,
        master_lanes,
        owner_lanes,
        owned_cells,
        cells,
        image,
        primal_cells,
        send_first,
        recv_first,
        send_ghost,
        recv_ghost,
        send_sub,
        recv_sub,
        send_sem,
        recv_sem,
        load_sem,
    ) = refs
    me = lax.axis_index("dom")
    count = lax.axis_size("dom")

    def exists(offset):
        other = me + offset
        return jnp.logical_and(other >= 0, other < count)

    barrier = pltpu.get_barrier_semaphore()
    for offset in OFFSETS:

        @pl.when(exists(offset))
        def _(offset=offset):
            pl.semaphore_signal(
                barrier, inc=1, device_id=(me + offset,), device_id_type=MESH
            )

    loads = [
        pltpu.make_async_copy(operands[k], staged[k], load_sem.at[k]) for k in range(15)
    ]
    for k in (11, 0, 3, 7, 8, 9, 10, 1, 2, 6, 5, 12, 13, 14, 4):
        loads[k].start()

    sent = []

    def exchange(send, recv, turn, direction, ready=None):
        copies = []
        for slot in FAR_FIRST:
            if ready is not None:
                ready(slot)
            away = direction * OFFSETS[slot]
            copy = pltpu.make_async_remote_copy(
                src_ref=send.at[slot],
                dst_ref=recv.at[slot],
                send_sem=send_sem.at[turn, slot],
                recv_sem=recv_sem.at[turn, slot],
                device_id=(me + away,),
                device_id_type=MESH,
            )
            pl.when(exists(away))(copy.start)
            copies.append((-away, copy))
            sent.append((away, copy))
        return copies

    def finish(copies):
        for away, copy in copies:
            pl.when(exists(away))(copy.wait_recv)

    for slot, offset in enumerate(OFFSETS):

        @pl.when(jnp.logical_not(exists(-offset)))
        def _(slot=slot):
            recv_first[slot] = jnp.zeros((12, LANES), F32)
            recv_sub[slot] = jnp.zeros((1, LANES), F32)
            for turn in range(SWEEPS):
                recv_ghost[2 * turn + 1, slot] = jnp.zeros((6, LANES), F32)

        @pl.when(jnp.logical_not(exists(offset)))
        def _(slot=slot):
            for turn in range(SWEEPS):
                recv_ghost[2 * turn, slot] = jnp.zeros((6, LANES), F32)

    def fill(ref, values):
        for part in range(3):
            low = part * STRIDE
            ref[low + OWNED - 6 : low + STRIDE, :] = jnp.zeros((STRIDE - OWNED + 6, LANES), F32)
            for row in range(OWNED):
                ref[low + row : low + row + 1, :] = values[
                    part : part + 1, row * LANES : (row + 1) * LANES
                ]

    def owned_rows(ref):
        def row_of(row):
            return lambda part: ref[part * STRIDE + row : part * STRIDE + row + 1, :]

        return [(row, row_of(row)) for row in range(OWNED)]

    def ghost_rows(recv, first=0):
        def row_of(row):
            spot = row % 2
            return lambda part: recv[
                row // 2, 2 * (first + part) + spot : 2 * (first + part) + spot + 1, :
            ]

        return [(STRIDE + row, row_of(row)) for row in range(GHOSTS)]

    lane_ids = lax.broadcasted_iota(jnp.int32, (SLOTS, 256), 1)
    loads[11].wait()
    lists = modulo(17 * lists_ref[...] + lane_ids, NODES_DEV)
    list_spots = [
        (lists[:, LANES * half : LANES * (half + 1)] >> 7, lists[:, LANES * half : LANES * (half + 1)] & 127)
        for half in range(2)
    ]
    loads[0].wait()
    fill(table, start_ref)

    def export(ref, send, first=0):
        found = looked_up(owned_rows(ref), list_spots, 3)
        for part in range(3):
            for half in range(2):
                spot = 2 * (first + part) + half
                for slot in range(SLOTS):
                    send[slot, spot : spot + 1, :] = found[half][part][slot : slot + 1]

    export(table, send_first)
    loads[3].wait()
    fill(primal_table, primal_ref)
    export(primal_table, send_first, 3)

    for k in (7, 8, 9, 10):
        loads[k].wait()
    node = node_ref[...]
    spots = modulo(13 * node, NODES_DEV)
    hang_row = jnp.where(node == PAD_CODE, -1, spots >> 7)
    numbers = (lax.broadcasted_iota(jnp.int32, (1, LANES), 1) + 1).astype(F32)
    source[: STRIDE, :] = dot_nt(
        (one_hot(hang_row, STRIDE, F32) * numbers).astype(BF16),
        one_hot(spots & 127, LANES, BF16),
    )

    def build(block, carry):
        span = pl.ds(pl.multiple_of(block * 8, 8), 8)
        codes = connect_ref[span, :]
        rows, lanes = place(modulo(17 * codes + 27 * lane_ids, EXT))
        pairs = [(rows[:, :LANES], lanes[:, :LANES]), (rows[:, LANES:], lanes[:, LANES:])]
        number = [each[0] for each in looked_up(owned_rows(source), pairs, 1)]
        number = jnp.concatenate(number, 1).astype(jnp.int32)
        rows = jnp.where(number > 0, HANG_ROW, rows)
        lanes = jnp.where(number > 0, number - 1, lanes)
        cell_rows[span, :] = rows
        cell_lanes[span, :] = lanes
        hang_hots[span, :] = jnp.where(rows == HANG_ROW, 1.0, 0.0)
        return carry

    lax.fori_loop(0, 8, build, 0)

    def build_hots(block):
        span = pl.ds(pl.multiple_of(block * 8, 8), 8)
        rows, lanes = cell_rows[span, :], cell_lanes[span, :]
        for step in range(8):
            spot = pl.ds(step * 256, 256)
            lane_hots[block, :, spot] = one_hot(lanes[step : step + 1], LANES, BF16)
            row_hots[block, :, spot] = one_hot(rows[step : step + 1], STRIDE, BF16)
            ghost_hots[block, :, spot] = one_hot(rows[step : step + 1], GHOSTS, F32, STRIDE)

    def gather_block(rows_of, base, out, block, blocks=1):
        spots, spans = [], []
        for step in range(blocks):
            low = pl.multiple_of((block * blocks + step) * 8, 8)
            for half in range(2):
                lane = pl.ds(half * LANES, LANES)
                spots.append((cell_rows[pl.ds(low, 8), lane], cell_lanes[pl.ds(low, 8), lane]))
                spans.append((low, lane))

        def span(part, where):
            return pl.ds(pl.multiple_of(part * 64 + where[0], 8), 8), where[1]

        start = None
        if base is not None:
            start = [[base[span(part, where)] for part in range(3)] for where in spans]
        found = looked_up(rows_of, spots, 3, start)
        for values, where in zip(found, spans):
            for part in range(3):
                out[span(part, where)] = values[part]

    def build_and_gather(block, carry):
        build_hots(block)
        gather_block(owned_rows(table), None, owned_cells, block)
        return carry

    lax.fori_loop(0, BUILD_FIRST, build_and_gather, 0)
    peers = jnp.minimum(me, REACH) + jnp.minimum(count - 1 - me, REACH)
    pl.semaphore_wait(barrier, peers)
    pending = exchange(send_first, recv_first, 0, 1)
    lax.fori_loop(BUILD_FIRST, 8, build_and_gather, 0)

    hang_ids = lax.broadcasted_iota(jnp.int32, (16, LANES), 1)
    rows, lanes = place(modulo(17 * master_ref[...] + 8 * hang_ids, EXT))
    weight = weight_ref[...]
    master_spots = [(rows[:8], lanes[:8]), (rows[8:], lanes[8:])]
    for step in range(16):
        spot = pl.ds(step * LANES, LANES)
        master_lanes[:, spot] = one_hot(lanes[step : step + 1], LANES, BF16)
        master_hots[:, spot] = (
            one_hot(rows[step : step + 1], STRIDE + GHOSTS, F32) * weight[step : step + 1]
        )

    def hanging(found):
        rows = []
        for part in range(3):
            total = found[0][part] * weight[:8] + found[1][part] * weight[8:]
            rows.append(jnp.sum(total, axis=0, keepdims=True))
        return rows

    def hang_rows(values):
        return [(HANG_ROW, lambda part: values[part])]

    def gather_cells(rows_of, base, out, blocks):
        def body(group, carry):
            gather_block(rows_of, base, out, group, blocks)
            return carry

        lax.fori_loop(0, 8 // blocks, body, 0)

    def image_rows(block):
        return [
            image[pl.ds(pl.multiple_of(part * 64 + block * 8, 8), 8), :] for part in range(3)
        ]

    def scatter_ghosts():
        def body(block, total):
            columns = []
            rows = image_rows(block)
            hang_hot = hang_hots[pl.ds(pl.multiple_of(block * 8, 8), 8), :]
            hung = [each * hang_hot for each in rows]
            for step in range(8):
                spot = pl.ds(step * 256, 256)
                ghost_hot = ghost_hots[block, :, spot]
                columns.append(
                    halves(
                        jnp.concatenate(
                            [each[step : step + 1] * ghost_hot for each in rows]
                            + [each[step : step + 1] for each in hung]
                            + [jnp.zeros((5, 256), F32)],
                            0,
                        )
                    )
                )
            return total + dot_nt(jnp.concatenate(columns, 1), lane_hots[block])

        zero = jnp.zeros((2 * (3 * GHOSTS + 8), LANES), F32)
        return joined(lax.fori_loop(0, 8, body, zero))

    def scatter_owned(beside=None):
        def body(block, total):
            if beside is not None:
                beside(block)
            columns = []
            rows = image_rows(block)
            values = split_rows(rows)
            for step in range(8):
                spot = pl.ds(step * 256, 256)
                columns.append(
                    spread_whole(
                        [each[step : step + 1] for each in values], row_hots[block, :, spot]
                    )
                )
            return total + dot_nt(jnp.concatenate(columns, 1), lane_hots[block])

        return joined(lax.fori_loop(0, 8, body, jnp.zeros((6 * STRIDE, LANES), F32)))

    def released(held, low, rows):
        columns = []
        for step in range(8):
            spot = pl.ds(step * 256, 256)
            columns.append(spread(held, master_hots[low : low + rows, spot]))
        return joined(dot_nt(jnp.concatenate(columns, 1), master_lanes[...]))

    def product(values, form):
        high = values.astype(BF16)
        low = (values - high.astype(F32)).astype(BF16)
        return form(stiff_high, high) + form(stiff_high, low) + form(stiff_low, high)

    owned_masters = looked_up(owned_rows(table), master_spots, 3)
    for k in (1, 2, 6, 5):
        loads[k].wait()
    stiff = stiff_ref[...]
    stiff_high = stiff.astype(BF16)
    stiff_low = (stiff - stiff_high.astype(F32)).astype(BF16)
    modulus = modulus_ref[...]
    fill(source, source_ref)
    fill(inverse, inverse_ref)
    for slot in range(SLOTS):
        row = lists[slot : slot + 1]
        spot = pl.ds(slot * 256, 256)
        list_lanes[:, spot] = one_hot(row & 127, LANES, BF16)
        list_hots[:, spot] = one_hot(row >> 7, STRIDE, BF16)

    recv, first = recv_first, 0
    for sweep in range(SWEEPS):
        finish(pending)
        hung = hanging(looked_up(ghost_rows(recv), master_spots, 3, owned_masters))
        gather_cells(ghost_rows(recv) + hang_rows(hung), owned_cells, cells, 8)
        image[...] = modulus * product(cells[...], dot_tn)
        totals = scatter_ghosts()
        held = [
            jnp.concatenate([totals[3 * GHOSTS + part : 3 * GHOSTS + part + 1]] * 2, 1)
            for part in range(3)
        ]
        totals = totals[: 3 * GHOSTS] + released(held, STRIDE, GHOSTS)
        send, recv = send_ghost.at[2 * sweep], recv_ghost.at[2 * sweep]

        def ready(slot, send=send, totals=totals):
            for part in range(3):
                spot = part * GHOSTS + 2 * slot
                send[slot, 2 * part : 2 * part + 2, :] = totals[spot : spot + 2]

        pending = exchange(send, recv, 2 * sweep + 1, -1, ready)

        beside = None
        if sweep == 0:
            primal_rows = owned_rows(primal_table) + ghost_rows(recv_first, 3)
            primal_rows += hang_rows(hanging(looked_up(primal_rows, master_spots, 3)))
            beside = functools.partial(gather_block, primal_rows, None, primal_cells)
        totals = scatter_owned(beside) + released(held, 0, STRIDE)
        if sweep == SWEEPS - 1:
            primal_cells[...] = modulus * product(primal_cells[...], dot)
            for k in (12, 13, 14):
                loads[k].wait()
            for slot in range(SLOTS):
                owner_lanes[:, pl.ds(slot * LANES, LANES)] = one_hot(
                    sub_owner_ref[slot : slot + 1, :], 256, BF16
                )
        finish(pending)
        columns = []
        for slot in range(SLOTS):
            rows = [
                jnp.concatenate(
                    [recv[slot, 2 * part : 2 * part + 1, :], recv[slot, 2 * part + 1 : 2 * part + 2, :]],
                    1,
                )
                for part in range(3)
            ]
            columns.append(
                spread_whole(split_rows(rows), list_hots[:, pl.ds(slot * 256, 256)])
            )
        returned = joined(dot_nt(jnp.concatenate(columns, 1), list_lanes[...]))
        table[...] = table[...] + RELAXATION * inverse[...] * (
            source[...] - (totals + returned)
        )
        send, recv = send_ghost.at[2 * sweep + 1], recv_ghost.at[2 * sweep + 1]
        export(table, send)
        pending = exchange(send, recv, 2 * sweep + 2, 1)

        owned_masters = looked_up(owned_rows(table), master_spots, 3)
        gather_cells(owned_rows(table), None, owned_cells, 2)

    for part in range(3):
        for row in range(OWNED):
            spot = part * STRIDE + row
            adjoint_ref[part : part + 1, row * LANES : (row + 1) * LANES] = table[
                spot : spot + 1, :
            ]
    loads[4].wait()
    face = lax.broadcasted_iota(jnp.int32, (16, 192), 0)
    node_id = lax.broadcasted_iota(jnp.int32, (16, 192), 1) & 63
    first, second, third = node_id >> 4, (node_id >> 2) & 3, node_id & 3
    axis_index = jnp.where(face < 2, first, jnp.where(face < 4, second, third))
    on_face = jnp.logical_and(face < 6, axis_index == 3 * (face & 1))
    faces = jnp.where(on_face, 1.0, 0.0).astype(BF16)
    sub_cell = sub_cell_ref[...]
    sub_spot = (2 * sub_face_ref[...] + (sub_cell >> 7), sub_cell & 127)

    finish(pending)
    hung = hanging(looked_up(ghost_rows(recv), master_spots, 3, owned_masters))
    gather_cells(ghost_rows(recv) + hang_rows(hung), owned_cells, cells, 8)
    applied = primal_cells[...]
    work = applied * cells[...]
    work_high = work.astype(BF16)
    work_low = (work - work_high.astype(F32)).astype(BF16)
    flux = dot(faces, work_high) + dot(faces, work_low)

    def flux_row(face, half):
        return lambda part: flux[face : face + 1, half * LANES : (half + 1) * LANES]

    flux_rows = [(2 * face + half, flux_row(face, half)) for face in range(6) for half in range(2)]
    found = looked_up(flux_rows, [sub_spot], 1)[0][0]
    for slot in range(SLOTS):
        send_sub[slot] = found[slot : slot + 1]
    pending = exchange(send_sub, recv_sub, 2 * SWEEPS + 1, 1)
    cell_term = jnp.sum(cells[...] * (load_ref[...] - applied), axis=0, keepdims=True)
    finish(pending)
    received = jnp.concatenate([recv_sub[slot] for slot in range(SLOTS)], 1)
    stacked = halves(jnp.broadcast_to(received, (8, SLOTS * LANES)))
    face_term = dot_nt(stacked, owner_lanes[...])
    face_term = face_term[0:1] + face_term[8:9]
    indicator_ref[...] = (jnp.abs(cell_term) + jnp.abs(face_term)) * (1.0 / 16.0)
    for away, copy in sent:
        pl.when(exists(away))(copy.wait_send)


def local(
    adjoint_start,
    adjoint_source,
    inverse_diagonal,
    primal_field,
    cell_load,
    modulus,
    stiffness,
    connectivity,
    hang_node,
    hang_master,
    hang_weight,
    ghost_lists,
    subface_cell,
    subface_face,
    subface_owner,
):
    turns = 2 * SWEEPS + 2
    operands = (
        adjoint_start,
        adjoint_source,
        inverse_diagonal,
        primal_field,
        cell_load,
        modulus.reshape(1, 256),
        stiffness,
        connectivity,
        hang_node.reshape(1, 128),
        hang_master,
        hang_weight,
        ghost_lists,
        subface_cell,
        subface_face,
        subface_owner,
    )
    vmem = pltpu.VMEM
    adjoint, indicator = pl.pallas_call(
        kernel,
        out_shape=(
            jax.ShapeDtypeStruct((3, NODES_DEV), F32),
            jax.ShapeDtypeStruct((1, 256), F32),
        ),
        in_specs=[pl.BlockSpec(memory_space=pl.ANY)] * 15,
        out_specs=(pl.BlockSpec(memory_space=pltpu.VMEM),) * 2,
        scratch_shapes=[vmem(each.shape, each.dtype) for each in operands]
        + [
            vmem((3 * STRIDE, LANES), F32),
            vmem((3 * STRIDE, LANES), F32),
            vmem((3 * STRIDE, LANES), F32),
            vmem((3 * STRIDE, LANES), F32),
            vmem((8, STRIDE, 8 * 256), BF16),
            vmem((8, GHOSTS, 8 * 256), F32),
            vmem((64, 256), F32),
            vmem((8, LANES, 8 * 256), BF16),
            vmem((64, 256), jnp.int32),
            vmem((64, 256), jnp.int32),
            vmem((STRIDE, SLOTS * 256), BF16),
            vmem((LANES, SLOTS * 256), BF16),
            vmem((STRIDE + GHOSTS, 16 * LANES), F32),
            vmem((LANES, 16 * LANES), BF16),
            vmem((256, SLOTS * LANES), BF16),
            vmem((192, 256), F32),
            vmem((192, 256), F32),
            vmem((192, 256), F32),
            vmem((192, 256), F32),
            vmem((SLOTS, 12, LANES), F32),
            vmem((SLOTS, 12, LANES), F32),
            vmem((2 * SWEEPS, SLOTS, 6, LANES), F32),
            vmem((2 * SWEEPS, SLOTS, 6, LANES), F32),
            vmem((SLOTS, 1, LANES), F32),
            vmem((SLOTS, 1, LANES), F32),
            pltpu.SemaphoreType.DMA((turns, SLOTS)),
            pltpu.SemaphoreType.DMA((turns, SLOTS)),
            pltpu.SemaphoreType.DMA((15,)),
        ],
        compiler_params=pltpu.CompilerParams(
            collective_id=0, has_side_effects=True, vmem_limit_bytes=56 * 1024 * 1024
        ),
    )(*operands)
    return adjoint, indicator.reshape(256)


def solution(mesh):
    wide, flat = P(None, "dom"), P("dom")
    placed = (wide,) * 5 + (flat, P(), wide, flat) + (wide,) * 6
    return jax.shard_map(
        local, mesh=mesh, in_specs=placed, out_specs=(wide, flat), check_vma=False
    )
```
